32 devices in a mesh: fsdp: 8 (over z, x), tp: 4 (over y, core).
Axes of the slice: x: 2, y: 2, z: 4, core: 2. Of those that a mesh axis runs over, the one named last changes fastest.
Arguments:
- gradients: bfloat16 [2, 2048, 8192], P(None, 'fsdp', 'tp'), may hold values from -120 to 120
- row_counts: int32 [8], replicated, may hold values from 128 to 256, as said below
- block_owner: int32 [2, 8], replicated, may hold values from 0 to 7, as said below
Outputs:
- update: bfloat16 [2, 2048, 8192], P(None, 'fsdp', 'tp')
- owned: bfloat16 [8192, 4096], P('fsdp', 'tp')
The draws below stay inside these ranges and needn't reach their ends.
Inputs may be any that keep to these rules, and one draw needn't show every extreme that they name: `row_counts`: every count is a multiple of 128; some index holds exactly 256. `block_owner`: blocks whose columns lie on the same tp index have distinct owners.
All inputs are finite; a program needn't handle non-finite values.
Results may differ from the reference program's by a relative error of at most 0.005.
The reference program's roundings to bfloat16 on the way count: a program that leaves them out, or rounds other values in their place, can miss the bound.
Values may be sent and summed in bfloat16 or wider, within the bound.
A program may use at most 128 MiB of HBM per device.

```python
import jax
import jax.numpy as jnp
from jax import lax

D = 8192
BLOCK = 1024
GRAIN = 128
LAYERS = 2
ROW_CAP = 256
ROWS = 2048
N_FSDP = 8
N_TP = 4


group_width = 32


def draw_gradients(key, part):
    keys = jax.random.split(jax.random.fold_in(key, 7), 6)
    group_total = D // group_width
    per_block = BLOCK // group_width
    member_list = []
    for block_index in range(D // BLOCK):
        shuffled = jax.random.permutation(jax.random.fold_in(keys[5], 40 + block_index), BLOCK)
        member_list.append(shuffled % per_block + block_index * per_block)
    membership = jnp.concatenate(member_list).astype(jnp.int32)
    independent = jnp.clip(jax.random.normal(keys[0], (LAYERS, ROWS, D), jnp.float32), -4.0, 4.0)
    common = jnp.clip(jax.random.normal(keys[1], (LAYERS, ROWS, group_total), jnp.float32), -4.0, 4.0)
    row_scale = jnp.exp(jax.random.uniform(keys[2], (LAYERS, ROWS, 1), jnp.float32, -1.15, 1.15))
    group_scale = jnp.exp(jax.random.uniform(keys[3], (LAYERS, 1, group_total), jnp.float32, -1.15, 1.15))
    spread_common = jnp.take(common, membership, axis=2)
    col_scale = jnp.take(group_scale, membership, axis=2)
    noise = 0.4 * independent + 0.92 * spread_common
    return (noise * row_scale * col_scale).astype(jnp.bfloat16)


def draw_row_counts(key, part):
    keys = jax.random.split(jax.random.fold_in(key, 19), 2)
    grains = jax.random.randint(keys[0], (N_FSDP,), 1, ROW_CAP // GRAIN + 1)
    fullest = jax.random.randint(keys[1], (), 0, N_FSDP)
    return jnp.where(jnp.arange(N_FSDP) == fullest, ROW_CAP, grains * GRAIN).astype(jnp.int32)


def draw_block_owner(key, part):
    per_group = D // (BLOCK * N_TP)
    columns = []
    for tp_group in range(N_TP):
        shuffled = jax.random.permutation(jax.random.fold_in(key, 300 + tp_group), N_FSDP)
        columns.append(shuffled[:LAYERS * per_group].reshape(LAYERS, per_group))
    return jnp.concatenate(columns, axis=1).astype(jnp.int32)


def setup_inputs(seed: int = 0) -> dict:
    key_list = jax.random.split(jax.random.key(seed), 4)
    gradients = draw_gradients(jax.random.fold_in(key_list[3], 71), 0)
    row_counts = draw_row_counts(jax.random.fold_in(key_list[3], 71), 0)
    block_owner = draw_block_owner(jax.random.fold_in(key_list[3], 71), 0)
    return {"gradients": gradients, "row_counts": row_counts, "block_owner": block_owner}


damping = 0.01

def newton_root(statistic):
    identity = jnp.eye(statistic.shape[0], dtype=jnp.float32)
    scaling = 2.5 / jnp.sqrt(jnp.sum(statistic * statistic))
    scaled = scaling * statistic
    factor_one = (5.0 * identity - scaled) / 4.0
    square = jnp.dot(factor_one, factor_one, precision=lax.Precision.HIGHEST)
    inner_part = jnp.dot(square, scaled, precision=lax.Precision.HIGHEST)
    contracted = jnp.dot(square, inner_part, precision=lax.Precision.HIGHEST)
    factor_two = (5.0 * identity - contracted) / 4.0
    result = jnp.dot(jnp.sqrt(jnp.sqrt(scaling)) * factor_one, factor_two, precision=lax.Precision.HIGHEST)
    return result.astype(jnp.bfloat16)

def gram_block(piece):
    widened = piece.astype(jnp.float32)
    return jnp.dot(widened.T, widened, precision=lax.Precision.HIGHEST)

def apply_block(paired):
    piece, root_block = paired
    return jnp.dot(piece, root_block, preferred_element_type=jnp.float32).astype(jnp.bfloat16)

def reference(gradients, row_counts, block_owner):
    positions = jnp.arange(ROWS, dtype=jnp.int32)
    limits = row_counts[positions // ROW_CAP]
    valid_rows = (positions % ROW_CAP < limits).astype(jnp.bfloat16)
    masked = gradients * valid_rows[None, :, None]
    total_rows = jnp.sum(row_counts).astype(jnp.float32)
    block_count = D // BLOCK
    per_group = block_count // N_TP
    identity = jnp.eye(BLOCK, dtype=jnp.float32)
    updates = []
    owned = jnp.zeros((N_FSDP, N_TP, BLOCK, BLOCK), jnp.bfloat16)
    for layer in range(LAYERS):
        blocked = jnp.transpose(masked[layer].reshape(ROWS, block_count, BLOCK), (1, 0, 2))
        grams = lax.map(gram_block, blocked)
        statistic = grams / total_rows + damping * identity
        root_list = lax.map(newton_root, statistic)
        applied = lax.map(apply_block, (blocked, root_list))
        updates.append(jnp.transpose(applied, (1, 0, 2)).reshape(ROWS, D))
        for column in range(block_count):
            owned = owned.at[block_owner[layer, column], column // per_group].set(root_list[column])
    owned_flat = jnp.transpose(owned, (0, 2, 1, 3)).reshape(N_FSDP * BLOCK, N_TP * BLOCK)
    return (jnp.stack(updates), owned_flat)
```

```python
import functools

import jax
import jax.numpy as jnp
from jax import lax
from jax.experimental import pallas as pl
from jax.experimental.pallas import tpu as pltpu
from jax.sharding import PartitionSpec as P

BLOCK = 1024
damping = 0.01
TILE = 256
STRIP = 128
STRIPS = BLOCK // STRIP
TILES = BLOCK // TILE
MESH = pl.DeviceIdType.MESH


def eye_strip(row0, rows, columns):
    row = lax.broadcasted_iota(jnp.int32, (rows, columns), 0) + row0
    column = lax.broadcasted_iota(jnp.int32, (rows, columns), 1)
    return (row == column).astype(jnp.float32)


def dot(a, b):
    return jnp.dot(a, b, preferred_element_type=jnp.float32)


def nearest_order(total):
    return [sorted(range(total), key=lambda k: (abs(k - b), k)) for b in range(total)]


def kernel(n, total, tp_total, count_ref, mine_ref, g_ref, update_ref, owned_ref, rows, gram, wide,
           low_a, low_b, low_x, roots, in_send, in_recv, up_send, down_send, mate_send, root_recv):
    me = lax.axis_index("fsdp")
    tp = lax.axis_index("tp")
    stride = n // total
    lane = lax.rem(tp, stride)
    home = me // stride
    is_home = lax.rem(me, stride) == lane

    def to(device):
        return {"fsdp": device}

    barrier = pltpu.get_barrier_semaphore()

    @pl.loop(1, n)
    def _(d):
        pl.semaphore_signal(barrier, inc=1, device_id=to(lax.rem(me + d, n)), device_id_type=MESH)

    pl.semaphore_wait(barrier, n - 1)

    def row_copy(block, source, target):
        return pltpu.make_async_remote_copy(
            src_ref=g_ref.at[block], dst_ref=rows.at[source], send_sem=in_send.at[block],
            recv_sem=in_recv.at[source], device_id=to(target), device_id_type=MESH)

    for block in range(total):
        target = stride * block + lane

        @pl.when(me != target)
        def _():
            row_copy(block, me, target).start()

    def strip_copy(k, s, target, send_sem):
        piece = roots.at[k, pl.ds(s * STRIP, STRIP), pl.ds(0, (s + 1) * STRIP)]
        return pltpu.make_async_remote_copy(
            src_ref=piece, dst_ref=piece, send_sem=send_sem, recv_sem=root_recv.at[k, s],
            device_id=to(target), device_id_type=MESH)

    def up_copy(k, s):
        return strip_copy(k, s, me + stride, up_send.at[k, s])

    def down_copy(k, s):
        return strip_copy(k, s, me - stride, down_send.at[k, s])

    def mate_copy(m, k, s):
        mate = stride * home + lax.rem(lane + 1 + m, stride)
        return strip_copy(k, s, mate, mate_send.at[m, k, s])

    def pass_on(k, s):
        for m in range(stride - 1):
            mate_copy(m, k, s).start()

        @pl.when((k <= home) & (home < total - 1))
        def _():
            up_copy(k, s).start()

        @pl.when((k >= home) & (home > 0))
        def _():
            down_copy(k, s).start()

    @pl.when(is_home)
    def _():
        def add_rows(read, first):
            @pl.loop(0, TILES)
            def _(i):
                at = pl.ds(pl.multiple_of(i * TILE, TILE), TILE)
                term = lax.dot_general(read(at), read(slice(None)), (((0,), (0,)), ((), ())),
                                       preferred_element_type=jnp.float32)
                gram[at, :] = term if first else gram[at, :] + term

        add_rows(lambda at: g_ref[home, :, at], True)

        @pl.loop(1, n)
        def _(d):
            source = lax.rem(me + d, n)
            row_copy(home, source, me).wait_recv()
            add_rows(lambda at: rows[source, :, at], False)

        inverse = 1.0 / jnp.full((1, 1), count_ref[0], jnp.float32)

        def statistic(i, squares):
            row0 = pl.multiple_of(i * TILE, TILE)
            at = pl.ds(row0, TILE)
            value = gram[at, :] * inverse + damping * eye_strip(row0, TILE, BLOCK)
            gram[at, :] = value
            return squares + jnp.sum(value * value, axis=0, keepdims=True)

        squares = lax.fori_loop(0, TILES, statistic, jnp.zeros((1, BLOCK), jnp.float32))
        scaling = 2.5 / jnp.sqrt(jnp.sum(squares, axis=1, keepdims=True))
        quarter = jnp.sqrt(jnp.sqrt(scaling))

        @pl.loop(0, TILES)
        def _(i):
            at = pl.ds(pl.multiple_of(i * TILE, TILE), TILE)
            scaled = gram[at, :] * scaling
            gram[at, :] = scaled
            low_a[at, :] = scaled.astype(jnp.bfloat16)

        @pl.loop(0, TILES)
        def _(i):
            at = pl.ds(pl.multiple_of(i * TILE, TILE), TILE)
            second = dot(low_a[at, :], low_a[...])
            scaled = gram[at, :]
            low_b[at, :] = (second * 0.0625 - 0.625 * scaled).astype(jnp.bfloat16)
            value = 1.25 * scaled - 0.25 * second
            wide[at, :] = value
            low_x[at, :] = value.astype(jnp.bfloat16)

        @pl.loop(0, TILES)
        def _(i):
            at = pl.ds(pl.multiple_of(i * TILE, TILE), TILE)
            value = 1.5625 * wide[at, :] + dot(low_b[at, :], low_x[...])
            wide[at, :] = value
            low_a[at, :] = value.astype(jnp.bfloat16)

        for i in range(TILES):
            at = pl.ds(i * TILE, TILE)
            width = (i + 1) * TILE
            value = 1.5625 * wide[at, :width] + dot(low_b[at, :], low_a[:, :width])
            value = 1.5625 * eye_strip(i * TILE, TILE, width) - 0.3125 * gram[at, :width] - 0.25 * value
            roots[home, at, pl.ds(0, width)] = (quarter * value).astype(jnp.bfloat16)
            for s in range(i * TILE // STRIP, (i + 1) * TILE // STRIP):
                pass_on(home, s)

    owned_ref[...] = jnp.zeros_like(owned_ref)
    order = nearest_order(total)

    @pl.loop(0, total)
    def _(step):
        k = jnp.int32(0)
        for b in range(total):
            for i in range(total):
                k = jnp.where((home == b) & (step == i), order[b][i], k)

        @pl.when(jnp.logical_not(is_home & (step == 0)))
        def _():
            for s in range(STRIPS):
                strip_copy(k, s, me, up_send.at[k, s]).wait_recv()

                @pl.when(is_home)
                def _():
                    pass_on(k, s)

        def mirror(row0, column0, size):
            piece = roots[k, pl.ds(row0, size), pl.ds(column0, size)]
            turned = piece.astype(jnp.float32).T.astype(jnp.bfloat16)
            roots[k, pl.ds(column0, size), pl.ds(row0, size)] = turned

        for i in range(TILES):
            mirror(i * TILE + STRIP, i * TILE, STRIP)
            for j in range(i):
                mirror(i * TILE, j * TILE, TILE)
        mine = mine_ref[k]

        @pl.loop(0, TILES)
        def _(i):
            at = pl.ds(pl.multiple_of(i * TILE, TILE), TILE)
            update_ref[k, :, at] = dot(g_ref[k], roots[k, :, at]).astype(jnp.bfloat16)
            held = owned_ref[at, :].astype(jnp.float32) + roots[k, at, :].astype(jnp.float32) * mine
            owned_ref[at, :] = held.astype(jnp.bfloat16)

    for block in range(total):
        target = stride * block + lane

        @pl.when(me != target)
        def _():
            row_copy(block, me, target).wait_send()

    @pl.when(is_home)
    def _():
        @pl.loop(0, total)
        def _(k):
            for s in range(STRIPS):
                for m in range(stride - 1):
                    mate_copy(m, k, s).wait_send()

                @pl.when((k <= home) & (home < total - 1))
                def _():
                    up_copy(k, s).wait_send()

                @pl.when((k >= home) & (home > 0))
                def _():
                    down_copy(k, s).wait_send()


def body(n, tp_total, gradients, row_counts, block_owner):
    fsdp_index = lax.axis_index("fsdp")
    tp_index = lax.axis_index("tp")
    layers, row_slots, columns = gradients.shape
    per_device = columns // BLOCK
    total = layers * per_device
    stride = n // total
    limit = row_counts[fsdp_index]
    valid_rows = (jnp.arange(row_slots, dtype=jnp.int32) < limit).astype(jnp.bfloat16)
    masked = gradients * valid_rows[None, :, None]
    blocked = masked.reshape(layers, row_slots, per_device, BLOCK).transpose(0, 2, 1, 3)
    blocked = blocked.reshape(total, row_slots, BLOCK)
    total_rows = jnp.sum(row_counts).astype(jnp.float32).reshape(1)
    local_owner = lax.dynamic_slice(
        block_owner, (jnp.int32(0), tp_index * per_device), (layers, per_device)
    ).reshape(total)
    mine = (local_owner == fsdp_index).astype(jnp.float32)
    vmem = pl.BlockSpec(memory_space=pltpu.VMEM)
    smem = pl.BlockSpec(memory_space=pltpu.SMEM)
    square = (BLOCK, BLOCK)
    dma = pltpu.SemaphoreType.DMA
    update, owned = pl.pallas_call(
        functools.partial(kernel, n, total, tp_total),
        out_shape=(
            jax.ShapeDtypeStruct((total, row_slots, BLOCK), jnp.bfloat16),
            jax.ShapeDtypeStruct(square, jnp.bfloat16),
        ),
        in_specs=[smem, smem, vmem],
        out_specs=(vmem, vmem),
        scratch_shapes=[
            pltpu.VMEM((n, row_slots, BLOCK), jnp.bfloat16),
            pltpu.VMEM(square, jnp.float32),
            pltpu.VMEM(square, jnp.float32),
            pltpu.VMEM(square, jnp.bfloat16),
            pltpu.VMEM(square, jnp.bfloat16),
            pltpu.VMEM(square, jnp.bfloat16),
            pltpu.VMEM((total,) + square, jnp.bfloat16),
            dma((total,)),
            dma((n,)),
            dma((total, STRIPS)),
            dma((total, STRIPS)),
            dma((max(stride - 1, 1), total, STRIPS)),
            dma((total, STRIPS)),
        ],
        compiler_params=pltpu.CompilerParams(
            collective_id=0, has_side_effects=True, vmem_limit_bytes=56 * 2**20
        ),
    )(total_rows, mine, blocked)
    update = update.reshape(layers, per_device, row_slots, BLOCK).transpose(0, 2, 1, 3)
    return update.reshape(layers, row_slots, columns), owned


def solution(mesh):
    placed = (P(None, "fsdp", "tp"), P(), P())
    return jax.shard_map(
        functools.partial(body, mesh.shape["fsdp"], mesh.shape["tp"]),
        mesh=mesh,
        in_specs=placed,
        out_specs=(P(None, "fsdp", "tp"), P("fsdp", "tp")),
        check_vma=False,
    )
```

```python
import functools

import jax
import jax.numpy as jnp
from jax import lax
from jax.experimental import pallas as pl
from jax.experimental.pallas import tpu as pltpu
from jax.sharding import PartitionSpec as P

BLOCK = 1024
damping = 0.01
TILE = 256
STRIP = 128
STRIPS = BLOCK // STRIP
TILES = BLOCK // TILE
MESH = pl.DeviceIdType.MESH


def eye_strip(row0, rows, columns):
    row = lax.broadcasted_iota(jnp.int32, (rows, columns), 0) + row0
    column = lax.broadcasted_iota(jnp.int32, (rows, columns), 1)
    return (row == column).astype(jnp.float32)


def dot(a, b):
    return jnp.dot(a, b, preferred_element_type=jnp.float32)


def arrange(total):
    place = sorted(range(total), key=lambda p: (abs(2 * p - total + 1), p))
    early = place[: total // 2]
    order = [sorted(range(total), key=lambda p: (p not in early, abs(p - h), p)) for h in range(total)]
    return place, order


def pick(index, table):
    value = jnp.int32(table[0])
    for i, entry in enumerate(table[1:], 1):
        value = jnp.where(index == i, entry, value)
    return value


def kernel(n, total, count_ref, owner_ref, g_ref, update_ref, owned_ref, masked, rows, gram, wide,
           low_a, low_b, low_x, roots, in_send, in_recv, home_send, up_send, down_send, mate_send, root_recv):
    me = lax.axis_index("fsdp")
    tp = lax.axis_index("tp")
    layers, row_slots, columns = g_ref.shape
    per_device = columns // BLOCK
    half = row_slots // 2
    stride = n // total
    lane = lax.rem(tp, stride)
    relay = lax.rem(lane + 1, stride)
    home = me // stride
    is_home = lax.rem(me, stride) == lane
    is_relay = lax.rem(me, stride) == relay
    place, order = arrange(total)
    early = total // 2
    block_at = [place.index(p) for p in range(total)]
    home_block = pick(home, block_at)
    is_early = is_home & (home_block < early)

    def to(device):
        return {"fsdp": device}

    barrier = pltpu.get_barrier_semaphore()

    @pl.loop(1, n)
    def _(d):
        pl.semaphore_signal(barrier, inc=1, device_id=to(lax.rem(me + d, n)), device_id_type=MESH)

    limit = count_ref[me]
    valid = lax.broadcasted_iota(jnp.int32, (row_slots, BLOCK), 0) < limit
    valid = jnp.where(valid, 1.0, 0.0).astype(jnp.bfloat16)
    for block in range(total):
        column0 = block % per_device * BLOCK
        masked[block] = g_ref[block // per_device, :, column0:column0 + BLOCK] * valid

    pl.semaphore_wait(barrier, n - 1)

    def row_copy(block, part, source, target):
        return pltpu.make_async_remote_copy(
            src_ref=masked.at[block, pl.ds(part * half, half)],
            dst_ref=rows.at[part, pl.ds(pl.multiple_of(source * half, half), half)],
            send_sem=in_send.at[block, part],
            recv_sem=in_recv.at[part, source], device_id=to(target), device_id_type=MESH)

    def each_send(blocks, act):
        for part in range(2):
            for block in blocks:
                target = stride * place[block] + lane

                @pl.when(me != target)
                def _():
                    act(row_copy(block, part, me, target))

    def second_sends():
        each_send(range(early), lambda copy: copy.wait_send())
        each_send(range(early, total), lambda copy: copy.start())

    each_send(range(early), lambda copy: copy.start())

    @pl.when(jnp.logical_not(is_early))
    def _():
        second_sends()

    def strip_copy(k, s, target, send_sem):
        piece = roots.at[k, pl.ds(s * STRIP, STRIP), pl.ds(0, (s + 1) * STRIP)]
        return pltpu.make_async_remote_copy(
            src_ref=piece, dst_ref=piece, send_sem=send_sem, recv_sem=root_recv.at[k, s],
            device_id=to(target), device_id_type=MESH)

    def home_copy(s):
        return strip_copy(home, s, stride * home + relay, home_send.at[s])

    def each_pass(k, s, act):
        for m in range(stride - 1):
            mate = stride * home + lax.rem(relay + 1 + m, stride)
            copy = strip_copy(k, s, mate, mate_send.at[m, k, s])
            if m < stride - 2:
                act(copy)
            else:
                @pl.when(k != home)
                def _():
                    act(copy)

        @pl.when((k <= home) & (home < total - 1))
        def _():
            act(strip_copy(k, s, me + stride, up_send.at[k, s]))

        @pl.when((k >= home) & (home > 0))
        def _():
            act(strip_copy(k, s, me - stride, down_send.at[k, s]))

    @pl.when(is_home)
    def _():
        def add_rows(part):
            mine_at = pl.ds(pl.multiple_of(me * half, half), half)
            rows[part, mine_at, :] = masked[home_block, part * half:(part + 1) * half, :]

            @pl.loop(1, n)
            def _(d):
                source = lax.rem(me + d, n)
                row_copy(home_block, part, source, me).wait_recv()

            @pl.loop(0, TILES)
            def _(i):
                at = pl.ds(pl.multiple_of(i * TILE, TILE), TILE)
                term = lax.dot_general(rows[part, :, at], rows[part], (((0,), (0,)), ((), ())),
                                       preferred_element_type=jnp.float32)
                gram[at, :] = term if part == 0 else gram[at, :] + term

        add_rows(0)

        @pl.when(is_early)
        def _():
            second_sends()

        add_rows(1)
        count = count_ref[0]
        for i in range(1, n):
            count = count + count_ref[i]
        total_rows = jnp.full((1, 1), count, jnp.int32).astype(jnp.float32)
        inverse = 1.0 / total_rows

        def statistic(i, squares):
            row0 = pl.multiple_of(i * TILE, TILE)
            at = pl.ds(row0, TILE)
            value = gram[at, :] * inverse + damping * eye_strip(row0, TILE, BLOCK)
            gram[at, :] = value
            return squares + jnp.sum(value * value, axis=0, keepdims=True)

        squares = lax.fori_loop(0, TILES, statistic, jnp.zeros((1, BLOCK), jnp.float32))
        scaling = 2.5 / jnp.sqrt(jnp.sum(squares, axis=1, keepdims=True))
        quarter = jnp.sqrt(jnp.sqrt(scaling))

        @pl.loop(0, TILES)
        def _(i):
            at = pl.ds(pl.multiple_of(i * TILE, TILE), TILE)
            scaled = gram[at, :] * scaling
            gram[at, :] = scaled
            low_a[at, :] = scaled.astype(jnp.bfloat16)

        @pl.loop(0, TILES)
        def _(i):
            at = pl.ds(pl.multiple_of(i * TILE, TILE), TILE)
            second = dot(low_a[at, :], low_a[...])
            scaled = gram[at, :]
            low_b[at, :] = (second * 0.0625 - 0.625 * scaled).astype(jnp.bfloat16)
            value = 1.25 * scaled - 0.25 * second
            wide[at, :] = value
            low_x[at, :] = value.astype(jnp.bfloat16)

        @pl.loop(0, TILES)
        def _(i):
            at = pl.ds(pl.multiple_of(i * TILE, TILE), TILE)
            value = 1.5625 * wide[at, :] + dot(low_b[at, :], low_x[...])
            wide[at, :] = value
            low_a[at, :] = value.astype(jnp.bfloat16)

        for i in range(TILES):
            at = pl.ds(i * TILE, TILE)
            width = (i + 1) * TILE
            value = 1.5625 * wide[at, :width] + dot(low_b[at, :], low_a[:, :width])
            value = 1.5625 * eye_strip(i * TILE, TILE, width) - 0.3125 * gram[at, :width] - 0.25 * value
            roots[home, at, pl.ds(0, width)] = (quarter * value).astype(jnp.bfloat16)
            for s in range(i * TILE // STRIP, (i + 1) * TILE // STRIP):
                home_copy(s).start()

    owned_ref[...] = jnp.zeros_like(owned_ref)

    @pl.loop(0, total)
    def _(step):
        k = pick(home * total + step, [p for line in order for p in line])

        @pl.when(jnp.logical_not(is_home & (k == home)))
        def _():
            for s in range(STRIPS):
                strip_copy(k, s, me, home_send.at[s]).wait_recv()

                @pl.when(is_relay)
                def _():
                    each_pass(k, s, lambda copy: copy.start())

        def mirror(row0, column0, size):
            piece = roots[k, pl.ds(row0, size), pl.ds(column0, size)]
            turned = piece.astype(jnp.float32).T.astype(jnp.bfloat16)
            roots[k, pl.ds(column0, size), pl.ds(row0, size)] = turned

        for i in range(TILES):
            mirror(i * TILE + STRIP, i * TILE, STRIP)
            for j in range(i):
                mirror(i * TILE, j * TILE, TILE)
        block = pick(k, block_at)
        layer = block // per_device
        column = lax.rem(block, per_device)
        owner = owner_ref[layer, tp * per_device + column]
        mine = jnp.where(owner == me, 1.0, 0.0)

        @pl.loop(0, TILES)
        def _(i):
            at = pl.ds(pl.multiple_of(i * TILE, TILE), TILE)
            out_at = pl.ds(pl.multiple_of(column * BLOCK + i * TILE, TILE), TILE)
            update_ref[layer, :, out_at] = dot(masked[block], roots[k, :, at]).astype(jnp.bfloat16)
            held = owned_ref[at, :].astype(jnp.float32) + roots[k, at, :].astype(jnp.float32) * mine
            owned_ref[at, :] = held.astype(jnp.bfloat16)

    each_send(range(early, total), lambda copy: copy.wait_send())

    @pl.when(is_home)
    def _():
        for s in range(STRIPS):
            home_copy(s).wait_send()

    @pl.when(is_relay)
    def _():
        @pl.loop(0, total)
        def _(k):
            for s in range(STRIPS):
                each_pass(k, s, lambda copy: copy.wait_send())


def body(n, gradients, row_counts, block_owner):
    layers, row_slots, columns = gradients.shape
    total = layers * (columns // BLOCK)
    stride = n // total
    vmem = pl.BlockSpec(memory_space=pltpu.VMEM)
    smem = pl.BlockSpec(memory_space=pltpu.SMEM)
    square = (BLOCK, BLOCK)
    dma = pltpu.SemaphoreType.DMA
    return pl.pallas_call(
        functools.partial(kernel, n, total),
        out_shape=(
            jax.ShapeDtypeStruct(gradients.shape, jnp.bfloat16),
            jax.ShapeDtypeStruct(square, jnp.bfloat16),
        ),
        in_specs=[smem, smem, vmem],
        out_specs=(vmem, vmem),
        scratch_shapes=[
            pltpu.VMEM((total, row_slots, BLOCK), jnp.bfloat16),
            pltpu.VMEM((2, n * row_slots // 2, BLOCK), jnp.bfloat16),
            pltpu.VMEM(square, jnp.float32),
            pltpu.VMEM(square, jnp.float32),
            pltpu.VMEM(square, jnp.bfloat16),
            pltpu.VMEM(square, jnp.bfloat16),
            pltpu.VMEM(square, jnp.bfloat16),
            pltpu.VMEM((total,) + square, jnp.bfloat16),
            dma((total, 2)),
            dma((2, n)),
            dma((STRIPS,)),
            dma((total, STRIPS)),
            dma((total, STRIPS)),
            dma((stride - 1, total, STRIPS)),
            dma((total, STRIPS)),
        ],
        compiler_params=pltpu.CompilerParams(
            collective_id=0, has_side_effects=True, vmem_limit_bytes=56 * 2**20
        ),
    )(row_counts, block_owner, gradients)


def solution(mesh):
    placed = (P(None, "fsdp", "tp"), P(), P())
    return jax.shard_map(
        functools.partial(body, mesh.shape["fsdp"]),
        mesh=mesh,
        in_specs=placed,
        out_specs=(P(None, "fsdp", "tp"), P("fsdp", "tp")),
        check_vma=False,
    )
```

```python
import functools

import jax
import jax.numpy as jnp
from jax import lax
from jax.experimental import pallas as pl
from jax.experimental.pallas import tpu as pltpu
from jax.sharding import PartitionSpec as P

BLOCK = 1024
damping = 0.01
TILE = 256
STRIP = 128
STRIPS = BLOCK // STRIP
TILES = BLOCK // TILE
CHUNK = 16
MESH = pl.DeviceIdType.MESH


def eye_strip(row0, rows, columns):
    row = lax.broadcasted_iota(jnp.int32, (rows, columns), 0) + row0
    column = lax.broadcasted_iota(jnp.int32, (rows, columns), 1)
    return (row == column).astype(jnp.float32)


def dot(a, b):
    return jnp.dot(a, b, preferred_element_type=jnp.float32)


def arrange(total):
    place = sorted(range(total), key=lambda p: (abs(2 * p - total + 1), p))
    early = place[: total // 2]
    order = [sorted(range(total), key=lambda p: (p not in early, abs(p - h), p)) for h in range(total)]
    return place, order


def pick(index, table):
    value = jnp.int32(table[0])
    for i, entry in enumerate(table[1:], 1):
        value = jnp.where(index == i, entry, value)
    return value


def kernel(n, total, count_ref, owner_ref, g_ref, update_ref, owned_ref, masked, rows, gram, wide,
           product, low_a, low_b, low_x, roots, in_send, in_recv, home_send, up_send, down_send, mate_send, root_recv):
    me = lax.axis_index("fsdp")
    tp = lax.axis_index("tp")
    layers, row_slots, columns = g_ref.shape
    per_device = columns // BLOCK
    half = row_slots // 2
    stride = n // total
    lane = lax.rem(tp, stride)
    relay = lax.rem(lane + 1, stride)
    home = me // stride
    is_home = lax.rem(me, stride) == lane
    is_relay = lax.rem(me, stride) == relay
    place, order = arrange(total)
    early = total // 2
    block_at = [place.index(p) for p in range(total)]
    home_block = pick(home, block_at)
    is_early = is_home & (home_block < early)

    def to(device):
        return {"fsdp": device}

    barrier = pltpu.get_barrier_semaphore()

    @pl.loop(1, n)
    def _(d):
        pl.semaphore_signal(barrier, inc=1, device_id=to(lax.rem(me + d, n)), device_id_type=MESH)

    limit = count_ref[me]

    @pl.loop(0, row_slots // CHUNK)
    def _(c):
        row0 = pl.multiple_of(c * CHUNK, CHUNK)
        at = pl.ds(row0, CHUNK)
        valid = lax.broadcasted_iota(jnp.int32, (CHUNK, BLOCK), 0) + row0 < limit
        valid = jnp.where(valid, 1.0, 0.0).astype(jnp.bfloat16)
        for block in range(total):
            column0 = block % per_device * BLOCK
            masked[block, at, :] = g_ref[block // per_device, at, column0:column0 + BLOCK] * valid

    pl.semaphore_wait(barrier, n - 1)

    def row_copy(block, part, source, target):
        return pltpu.make_async_remote_copy(
            src_ref=masked.at[block, pl.ds(part * half, half)],
            dst_ref=rows.at[part, pl.ds(pl.multiple_of(source * half, half), half)],
            send_sem=in_send.at[block, part],
            recv_sem=in_recv.at[part, source], device_id=to(target), device_id_type=MESH)

    def each_send(blocks, act):
        for part in range(2):
            for block in blocks:
                target = stride * place[block] + lane

                @pl.when(me != target)
                def _():
                    act(row_copy(block, part, me, target))

    def second_sends():
        each_send(range(early), lambda copy: copy.wait_send())
        each_send(range(early, total), lambda copy: copy.start())

    each_send(range(early), lambda copy: copy.start())

    @pl.when(jnp.logical_not(is_early))
    def _():
        second_sends()

    def strip_copy(k, s, target, send_sem):
        piece = roots.at[k, pl.ds(s * STRIP, STRIP), pl.ds(0, (s + 1) * STRIP)]
        return pltpu.make_async_remote_copy(
            src_ref=piece, dst_ref=piece, send_sem=send_sem, recv_sem=root_recv.at[k, s],
            device_id=to(target), device_id_type=MESH)

    def home_copy(s):
        return strip_copy(home, s, stride * home + relay, home_send.at[s])

    def each_pass(k, s, act):
        for m in range(stride - 1):
            mate = stride * home + lax.rem(relay + 1 + m, stride)
            copy = strip_copy(k, s, mate, mate_send.at[m, k, s])
            if m < stride - 2:
                act(copy)
            else:
                @pl.when(k != home)
                def _():
                    act(copy)

        @pl.when((k <= home) & (home < total - 1))
        def _():
            act(strip_copy(k, s, me + stride, up_send.at[k, s]))

        @pl.when((k >= home) & (home > 0))
        def _():
            act(strip_copy(k, s, me - stride, down_send.at[k, s]))

    @pl.when(is_home)
    def _():
        def take_rows(part):
            mine_at = pl.ds(pl.multiple_of(me * half, half), half)
            rows[part, mine_at, :] = masked[home_block, part * half:(part + 1) * half, :]

            @pl.loop(1, n)
            def _(d):
                source = lax.rem(me + d, n)
                row_copy(home_block, part, source, me).wait_recv()

        def gram_strip(part, at):
            return lax.dot_general(rows[part, :, at], rows[part], (((0,), (0,)), ((), ())),
                                   preferred_element_type=jnp.float32)

        def strips(act, start=0):
            return lax.fori_loop(0, TILES, lambda i, x: act(pl.multiple_of(i * TILE, TILE), x), start)

        def chunks(row0, act, start=0):
            def step(c, x):
                first = pl.multiple_of(c * CHUNK, CHUNK)
                return act(pl.ds(first, CHUNK), pl.ds(pl.multiple_of(row0 + first, CHUNK), CHUNK), x)

            return lax.fori_loop(0, TILE // CHUNK, step, start)

        take_rows(0)

        def first_half(row0, x):
            at = pl.ds(row0, TILE)
            gram[at, :] = gram_strip(0, at)
            return x

        strips(first_half)

        @pl.when(is_early)
        def _():
            second_sends()

        take_rows(1)
        count = count_ref[0]
        for i in range(1, n):
            count = count + count_ref[i]
        inverse = 1.0 / jnp.full((1, 1), count, jnp.int32).astype(jnp.float32)

        def statistic(row0, squares):
            at = pl.ds(row0, TILE)
            product[...] = gram_strip(1, at)

            def step(near, far, squares):
                value = (gram[far, :] + product[near, :]) * inverse
                gram[far, :] = value
                low_a[far, :] = value.astype(jnp.bfloat16)
                value = value * value
                return squares + value[:8] + value[8:]

            squares = chunks(row0, step, squares)
            eye = eye_strip(0, TILE, TILE)
            value = gram[at, at]
            extra = eye * (2.0 * damping * value + damping * damping)
            value = value + damping * eye
            gram[at, at] = value
            low_a[at, at] = value.astype(jnp.bfloat16)
            extra = jnp.sum(extra.reshape(TILE // 8, 8, TILE), axis=0)
            return squares + jnp.concatenate([extra] + [jnp.zeros_like(extra)] * (TILES - 1), axis=1)

        squares = strips(statistic, jnp.zeros((8, BLOCK), jnp.float32))
        squares = jnp.sum(squares, axis=0, keepdims=True)
        scaling = 2.5 / jnp.sqrt(jnp.sum(squares, axis=1, keepdims=True))
        quarter = jnp.sqrt(jnp.sqrt(scaling))

        def second_power(row0, x):
            product[...] = dot(low_a[pl.ds(row0, TILE), :], low_a[...])

            def step(near, far, x):
                second = product[near, :] * (scaling * scaling)
                scaled = gram[far, :] * scaling
                gram[far, :] = scaled
                low_b[far, :] = (0.0625 * second - 0.625 * scaled).astype(jnp.bfloat16)
                value = 1.25 * scaled - 0.25 * second
                wide[far, :] = value
                low_x[far, :] = value.astype(jnp.bfloat16)
                return x

            return chunks(row0, step, x)

        strips(second_power)

        def third_power(row0, x):
            product[...] = dot(low_b[pl.ds(row0, TILE), :], low_x[...])

            def step(near, far, x):
                value = 1.5625 * wide[far, :] + product[near, :]
                wide[far, :] = value
                low_a[far, :] = value.astype(jnp.bfloat16)
                return x

            return chunks(row0, step, x)

        strips(third_power)

        for i in range(TILES):
            at = pl.ds(i * TILE, TILE)
            width = (i + 1) * TILE
            product[:, :width] = dot(low_b[at, :], low_a[:, :width])

            def step(near, far, x, width=width):
                value = 1.5625 * wide[far, :width] + product[near, :width]
                value = quarter * (-0.3125 * gram[far, :width] - 0.25 * value)
                wide[far, :width] = value
                roots[home, far, :width] = value.astype(jnp.bfloat16)
                return x

            chunks(i * TILE, step, 0)
            value = wide[at, at] + quarter * (1.5625 * eye_strip(0, TILE, TILE))
            roots[home, at, at] = value.astype(jnp.bfloat16)
            for s in range(i * TILE // STRIP, (i + 1) * TILE // STRIP):
                home_copy(s).start()

    owned_ref[...] = jnp.zeros_like(owned_ref)

    @pl.loop(0, total)
    def _(step):
        k = pick(home * total + step, [p for line in order for p in line])

        @pl.when(jnp.logical_not(is_home & (k == home)))
        def _():
            for s in range(STRIPS):
                strip_copy(k, s, me, home_send.at[s]).wait_recv()

                @pl.when(is_relay)
                def _():
                    each_pass(k, s, lambda copy: copy.start())

        def mirror(row0, column0, size):
            piece = roots[k, pl.ds(row0, size), pl.ds(column0, size)]
            roots[k, pl.ds(column0, size), pl.ds(row0, size)] = piece.T

        for i in range(TILES):
            mirror(i * TILE + STRIP, i * TILE, STRIP)
            for j in range(i):
                mirror(i * TILE, j * TILE, TILE)
        block = pick(k, block_at)
        layer = block // per_device
        column = lax.rem(block, per_device)
        owner = owner_ref[layer, tp * per_device + column]

        @pl.loop(0, TILES)
        def _(i):
            at = pl.ds(pl.multiple_of(i * TILE, TILE), TILE)
            out_at = pl.ds(pl.multiple_of(column * BLOCK + i * TILE, TILE), TILE)
            update_ref[layer, :, out_at] = dot(masked[block], roots[k, :, at]).astype(jnp.bfloat16)
            owned_ref[at, :] = jnp.where(owner == me, roots[k, at, :], owned_ref[at, :])

    each_send(range(early, total), lambda copy: copy.wait_send())

    @pl.when(is_home)
    def _():
        for s in range(STRIPS):
            home_copy(s).wait_send()

    @pl.when(is_relay)
    def _():
        @pl.loop(0, total)
        def _(k):
            for s in range(STRIPS):
                each_pass(k, s, lambda copy: copy.wait_send())


def body(n, gradients, row_counts, block_owner):
    layers, row_slots, columns = gradients.shape
    total = layers * (columns // BLOCK)
    stride = n // total
    vmem = pl.BlockSpec(memory_space=pltpu.VMEM)
    smem = pl.BlockSpec(memory_space=pltpu.SMEM)
    square = (BLOCK, BLOCK)
    dma = pltpu.SemaphoreType.DMA
    return pl.pallas_call(
        functools.partial(kernel, n, total),
        out_shape=(
            jax.ShapeDtypeStruct(gradients.shape, jnp.bfloat16),
            jax.ShapeDtypeStruct(square, jnp.bfloat16),
        ),
        in_specs=[smem, smem, vmem],
        out_specs=(vmem, vmem),
        scratch_shapes=[
            pltpu.VMEM((total, row_slots, BLOCK), jnp.bfloat16),
            pltpu.VMEM((2, n * row_slots // 2, BLOCK), jnp.bfloat16),
            pltpu.VMEM(square, jnp.float32),
            pltpu.VMEM(square, jnp.float32),
            pltpu.VMEM((TILE, BLOCK), jnp.float32),
            pltpu.VMEM(square, jnp.bfloat16),
            pltpu.VMEM(square, jnp.bfloat16),
            pltpu.VMEM(square, jnp.bfloat16),
            pltpu.VMEM((total,) + square, jnp.bfloat16),
            dma((total, 2)),
            dma((2, n)),
            dma((STRIPS,)),
            dma((total, STRIPS)),
            dma((total, STRIPS)),
            dma((stride - 1, total, STRIPS)),
            dma((total, STRIPS)),
        ],
        compiler_params=pltpu.CompilerParams(
            collective_id=0, has_side_effects=True, vmem_limit_bytes=56 * 2**20
        ),
    )(row_counts, block_owner, gradients)


def solution(mesh):
    placed = (P(None, "fsdp", "tp"), P(), P())
    return jax.shard_map(
        functools.partial(body, mesh.shape["fsdp"]),
        mesh=mesh,
        in_specs=placed,
        out_specs=(P(None, "fsdp", "tp"), P("fsdp", "tp")),
        check_vma=False,
    )
```

```python
import functools

import jax
import jax.numpy as jnp
from jax import lax
from jax.experimental import pallas as pl
from jax.experimental.pallas import tpu as pltpu
from jax.sharding import PartitionSpec as P

BLOCK = 1024
damping = 0.01
TILE = 256
STRIP = 128
STRIPS = BLOCK // STRIP
TILES = BLOCK // TILE
CHUNK = 16
DETOUR = (2, 6, 7)
MESH = pl.DeviceIdType.MESH


def eye_strip(row0, rows, columns):
    row = lax.broadcasted_iota(jnp.int32, (rows, columns), 0) + row0
    column = lax.broadcasted_iota(jnp.int32, (rows, columns), 1)
    return (row == column).astype(jnp.float32)


def dot(a, b):
    return jnp.dot(a, b, preferred_element_type=jnp.float32)


def pick(index, table):
    value = jnp.int32(table[0])
    for i, entry in enumerate(table[1:], 1):
        value = jnp.where(index == i, entry, value)
    return value


def kernel(n, total, count_ref, owner_ref, g_ref, update_ref, owned_ref, masked, rows, gram, wide,
           product, low_a, low_b, low_x, roots, in_send, in_recv, up_send, down_send, mate_send, root_recv):
    me = lax.axis_index("fsdp")
    tp = lax.axis_index("tp")
    layers, row_slots, columns = g_ref.shape
    per_device = columns // BLOCK
    half = row_slots // 2
    stride = n // total
    lane = lax.rem(tp, stride)
    beside = lax.rem(lane + 1, stride)
    home = me // stride
    is_home = lax.rem(me, stride) == lane
    is_beside = lax.rem(me, stride) == beside
    upper = home >= total // 2
    order = [sorted(range(total), key=lambda k: (abs(k - h), k)) for h in range(total)]

    def to(device):
        return {"fsdp": device}

    barrier = pltpu.get_barrier_semaphore()

    @pl.loop(1, n)
    def _(d):
        pl.semaphore_signal(barrier, inc=1, device_id=to(lax.rem(me + d, n)), device_id_type=MESH)

    limit = count_ref[me]

    @pl.loop(0, row_slots // CHUNK)
    def _(c):
        row0 = pl.multiple_of(c * CHUNK, CHUNK)
        at = pl.ds(row0, CHUNK)
        valid = lax.broadcasted_iota(jnp.int32, (CHUNK, BLOCK), 0) + row0 < limit
        valid = jnp.where(valid, 1.0, 0.0).astype(jnp.bfloat16)
        for block in range(total):
            column0 = block % per_device * BLOCK
            masked[block, at, :] = g_ref[block // per_device, at, column0:column0 + BLOCK] * valid

    pl.semaphore_wait(barrier, n - 1)

    def row_copy(block, part, source, target):
        return pltpu.make_async_remote_copy(
            src_ref=masked.at[block, pl.ds(part * half, half)],
            dst_ref=rows.at[part, pl.ds(pl.multiple_of(source * half, half), half)],
            send_sem=in_send.at[block, part],
            recv_sem=in_recv.at[part, source], device_id=to(target), device_id_type=MESH)

    def each_send(act):
        for part in range(2):
            for block in range(total):
                target = stride * block + lane

                @pl.when(me != target)
                def _():
                    act(row_copy(block, part, me, target))

    each_send(lambda copy: copy.start())

    def strip_copy(k, s, target, send_sem):
        piece = roots.at[k, pl.ds(s * STRIP, STRIP), pl.ds(0, (s + 1) * STRIP)]
        return pltpu.make_async_remote_copy(
            src_ref=piece, dst_ref=piece, send_sem=send_sem, recv_sem=root_recv.at[k, s],
            device_id=to(target), device_id_type=MESH)

    def up_copy(k, s):
        return strip_copy(k, s, me + stride, up_send.at[k, s])

    def down_copy(k, s):
        return strip_copy(k, s, me - stride, down_send.at[k, s])

    def along_chain(k):
        return (upper & (k == 0)) | (jnp.logical_not(upper) & (k == total - 1))

    def home_pass(k, s, act):
        @pl.when((k <= home) & (home < total - 1))
        def _():
            act(up_copy(k, s))

        @pl.when((k >= home) & (home > 0))
        def _():
            act(down_copy(k, s))

        for m in range(stride - 1):
            mate = stride * home + lax.rem(lane + 1 + m, stride)
            copy = strip_copy(k, s, mate, mate_send.at[m, k, s])
            if m == 0 and s in DETOUR:
                @pl.when(jnp.logical_not(along_chain(k)))
                def _():
                    act(copy)
            else:
                act(copy)

    def beside_pass(k, s, act):
        if s in DETOUR:
            @pl.when((k == 0) & (home >= total // 2 - 1) & (home < total - 1))
            def _():
                act(up_copy(k, s))

            @pl.when((k == total - 1) & (home <= total // 2) & (home > 0))
            def _():
                act(down_copy(k, s))

    @pl.when(is_home)
    def _():
        def take_rows(part):
            mine_at = pl.ds(pl.multiple_of(me * half, half), half)
            rows[part, mine_at, :] = masked[home, part * half:(part + 1) * half, :]

            @pl.loop(1, n)
            def _(d):
                source = lax.rem(me + d, n)
                row_copy(home, part, source, me).wait_recv()

        def gram_strip(part, at):
            return lax.dot_general(rows[part, :, at], rows[part], (((0,), (0,)), ((), ())),
                                   preferred_element_type=jnp.float32)

        def strips(act, start=0):
            return lax.fori_loop(0, TILES, lambda i, x: act(pl.multiple_of(i * TILE, TILE), x), start)

        def chunks(row0, act, start=0):
            def step(c, x):
                first = pl.multiple_of(c * CHUNK, CHUNK)
                return act(pl.ds(first, CHUNK), pl.ds(pl.multiple_of(row0 + first, CHUNK), CHUNK), x)

            return lax.fori_loop(0, TILE // CHUNK, step, start)

        take_rows(0)

        def first_half(row0, x):
            at = pl.ds(row0, TILE)
            gram[at, :] = gram_strip(0, at)
            return x

        strips(first_half)

        take_rows(1)
        count = count_ref[0]
        for i in range(1, n):
            count = count + count_ref[i]
        inverse = 1.0 / jnp.full((1, 1), count, jnp.int32).astype(jnp.float32)

        def statistic(row0, squares):
            at = pl.ds(row0, TILE)
            product[...] = gram_strip(1, at)

            def step(near, far, squares):
                value = (gram[far, :] + product[near, :]) * inverse
                gram[far, :] = value
                low_a[far, :] = value.astype(jnp.bfloat16)
                value = value * value
                return squares + value[:8] + value[8:]

            squares = chunks(row0, step, squares)
            eye = eye_strip(0, TILE, TILE)
            value = gram[at, at]
            extra = eye * (2.0 * damping * value + damping * damping)
            value = value + damping * eye
            gram[at, at] = value
            low_a[at, at] = value.astype(jnp.bfloat16)
            extra = jnp.sum(extra.reshape(TILE // 8, 8, TILE), axis=0)
            return squares + jnp.concatenate([extra] + [jnp.zeros_like(extra)] * (TILES - 1), axis=1)

        squares = strips(statistic, jnp.zeros((8, BLOCK), jnp.float32))
        squares = jnp.sum(squares, axis=0, keepdims=True)
        scaling = 2.5 / jnp.sqrt(jnp.sum(squares, axis=1, keepdims=True))
        quarter = jnp.sqrt(jnp.sqrt(scaling))

        def second_power(row0, x):
            product[...] = dot(low_a[pl.ds(row0, TILE), :], low_a[...])

            def step(near, far, x):
                second = product[near, :] * (scaling * scaling)
                scaled = gram[far, :] * scaling
                gram[far, :] = scaled
                low_b[far, :] = (0.0625 * second - 0.625 * scaled).astype(jnp.bfloat16)
                value = 1.25 * scaled - 0.25 * second
                wide[far, :] = value
                low_x[far, :] = value.astype(jnp.bfloat16)
                return x

            return chunks(row0, step, x)

        strips(second_power)

        def third_power(row0, x):
            product[...] = dot(low_b[pl.ds(row0, TILE), :], low_x[...])

            def step(near, far, x):
                value = 1.5625 * wide[far, :] + product[near, :]
                wide[far, :] = value
                low_a[far, :] = value.astype(jnp.bfloat16)
                return x

            return chunks(row0, step, x)

        strips(third_power)

        for i in range(TILES):
            at = pl.ds(i * TILE, TILE)
            width = (i + 1) * TILE
            product[:, :width] = dot(low_b[at, :], low_a[:, :width])

            def step(near, far, x, width=width):
                value = 1.5625 * wide[far, :width] + product[near, :width]
                value = quarter * (-0.3125 * gram[far, :width] - 0.25 * value)
                wide[far, :width] = value
                roots[home, far, :width] = value.astype(jnp.bfloat16)
                return x

            chunks(i * TILE, step, 0)
            value = wide[at, at] + quarter * (1.5625 * eye_strip(0, TILE, TILE))
            roots[home, at, at] = value.astype(jnp.bfloat16)
            for s in range(i * TILE // STRIP, (i + 1) * TILE // STRIP):
                home_pass(home, s, lambda copy: copy.start())

    owned_ref[...] = jnp.zeros_like(owned_ref)

    @pl.loop(0, total)
    def _(step):
        k = pick(home * total + step, [p for line in order for p in line])

        @pl.when(jnp.logical_not(is_home & (k == home)))
        def _():
            for s in range(STRIPS):
                strip_copy(k, s, me, up_send.at[k, s]).wait_recv()

                @pl.when(is_home)
                def _():
                    home_pass(k, s, lambda copy: copy.start())

                @pl.when(is_beside)
                def _():
                    beside_pass(k, s, lambda copy: copy.start())

        def mirror(row0, column0, size):
            piece = roots[k, pl.ds(row0, size), pl.ds(column0, size)]
            roots[k, pl.ds(column0, size), pl.ds(row0, size)] = piece.T

        for i in range(TILES):
            mirror(i * TILE + STRIP, i * TILE, STRIP)
            for j in range(i):
                mirror(i * TILE, j * TILE, TILE)
        layer = k // per_device
        column = lax.rem(k, per_device)
        owner = owner_ref[layer, tp * per_device + column]

        @pl.loop(0, TILES)
        def _(i):
            at = pl.ds(pl.multiple_of(i * TILE, TILE), TILE)
            out_at = pl.ds(pl.multiple_of(column * BLOCK + i * TILE, TILE), TILE)
            update_ref[layer, :, out_at] = dot(masked[k], roots[k, :, at]).astype(jnp.bfloat16)
            owned_ref[at, :] = jnp.where(owner == me, roots[k, at, :], owned_ref[at, :])

    each_send(lambda copy: copy.wait_send())

    @pl.loop(0, total)
    def _(k):
        for s in range(STRIPS):
            @pl.when(is_home)
            def _():
                home_pass(k, s, lambda copy: copy.wait_send())

            @pl.when(is_beside)
            def _():
                beside_pass(k, s, lambda copy: copy.wait_send())


def body(n, gradients, row_counts, block_owner):
    layers, row_slots, columns = gradients.shape
    total = layers * (columns // BLOCK)
    stride = n // total
    vmem = pl.BlockSpec(memory_space=pltpu.VMEM)
    smem = pl.BlockSpec(memory_space=pltpu.SMEM)
    square = (BLOCK, BLOCK)
    dma = pltpu.SemaphoreType.DMA
    return pl.pallas_call(
        functools.partial(kernel, n, total),
        out_shape=(
            jax.ShapeDtypeStruct(gradients.shape, jnp.bfloat16),
            jax.ShapeDtypeStruct(square, jnp.bfloat16),
        ),
        in_specs=[smem, smem, vmem],
        out_specs=(vmem, vmem),
        scratch_shapes=[
            pltpu.VMEM((total, row_slots, BLOCK), jnp.bfloat16),
            pltpu.VMEM((2, n * row_slots // 2, BLOCK), jnp.bfloat16),
            pltpu.VMEM(square, jnp.float32),
            pltpu.VMEM(square, jnp.float32),
            pltpu.VMEM((TILE, BLOCK), jnp.float32),
            pltpu.VMEM(square, jnp.bfloat16),
            pltpu.VMEM(square, jnp.bfloat16),
            pltpu.VMEM(square, jnp.bfloat16),
            pltpu.VMEM((total,) + square, jnp.bfloat16),
            dma((total, 2)),
            dma((2, n)),
            dma((total, STRIPS)),
            dma((total, STRIPS)),
            dma((stride - 1, total, STRIPS)),
            dma((total, STRIPS)),
        ],
        compiler_params=pltpu.CompilerParams(
            collective_id=0, has_side_effects=True, vmem_limit_bytes=56 * 2**20
        ),
    )(row_counts, block_owner, gradients)


def solution(mesh):
    placed = (P(None, "fsdp", "tp"), P(), P())
    return jax.shard_map(
        functools.partial(body, mesh.shape["fsdp"]),
        mesh=mesh,
        in_specs=placed,
        out_specs=(P(None, "fsdp", "tp"), P("fsdp", "tp")),
        check_vma=False,
    )
```

```python
import functools

import jax
import jax.numpy as jnp
from jax import lax
from jax.experimental import pallas as pl
from jax.experimental.pallas import tpu as pltpu
from jax.sharding import PartitionSpec as P

BLOCK = 1024
damping = 0.01
TILE = 256
STRIP = 128
STRIPS = BLOCK // STRIP
TILES = BLOCK // TILE
CHUNK = 16
DETOUR = (2, 6, 7)
MESH = pl.DeviceIdType.MESH


def eye_strip(row0, rows, columns):
    row = lax.broadcasted_iota(jnp.int32, (rows, columns), 0) + row0
    column = lax.broadcasted_iota(jnp.int32, (rows, columns), 1)
    return (row == column).astype(jnp.float32)


def dot(a, b):
    return jnp.dot(a, b, preferred_element_type=jnp.float32)


def pick(index, table):
    value = jnp.int32(table[0])
    for i, entry in enumerate(table[1:], 1):
        value = jnp.where(index == i, entry, value)
    return value


def kernel(n, total, count_ref, owner_ref, g_ref, update_ref, owned_ref, masked, rows, gram, wide,
           product, low_a, low_b, low_x, roots, in_send, in_recv, up_send, down_send, mate_send, root_recv):
    me = lax.axis_index("fsdp")
    tp = lax.axis_index("tp")
    layers, row_slots, columns = g_ref.shape
    per_device = columns // BLOCK
    half = row_slots // 2
    stride = n // total
    lane = lax.rem(tp, stride)
    beside = lax.rem(lane + 1, stride)
    home = me // stride
    is_home = lax.rem(me, stride) == lane
    is_beside = lax.rem(me, stride) == beside
    upper = home >= total // 2
    order = [sorted(range(total), key=lambda k: (abs(k - h), k)) for h in range(total)]

    def to(device):
        return {"fsdp": device}

    barrier = pltpu.get_barrier_semaphore()

    @pl.loop(1, n)
    def _(d):
        pl.semaphore_signal(barrier, inc=1, device_id=to(lax.rem(me + d, n)), device_id_type=MESH)

    limit = count_ref[me]

    @pl.loop(0, row_slots // CHUNK)
    def _(c):
        row0 = pl.multiple_of(c * CHUNK, CHUNK)
        at = pl.ds(row0, CHUNK)
        valid = lax.broadcasted_iota(jnp.int32, (CHUNK, BLOCK), 0) + row0 < limit
        valid = jnp.where(valid, 1.0, 0.0).astype(jnp.bfloat16)
        for block in range(total):
            column0 = block % per_device * BLOCK
            masked[block, at, :] = g_ref[block // per_device, at, column0:column0 + BLOCK] * valid

    pl.semaphore_wait(barrier, n - 1)

    def row_copy(block, part, source, target):
        return pltpu.make_async_remote_copy(
            src_ref=masked.at[block, pl.ds(part * half, half)],
            dst_ref=rows.at[part, pl.ds(pl.multiple_of(source * half, half), half)],
            send_sem=in_send.at[block, part],
            recv_sem=in_recv.at[part, source], device_id=to(target), device_id_type=MESH)

    def each_send(act):
        for part in range(2):
            for turn in sorted(range(total), key=lambda d: (d == 0, abs(2 * d - total), d)):
                block = lax.rem(home + turn, total)
                target = stride * block + lane

                @pl.when(me != target)
                def _():
                    act(row_copy(block, part, me, target))

    each_send(lambda copy: copy.start())

    def strip_copy(k, s, target, send_sem):
        piece = roots.at[k, pl.ds(s * STRIP, STRIP), pl.ds(0, (s + 1) * STRIP)]
        return pltpu.make_async_remote_copy(
            src_ref=piece, dst_ref=piece, send_sem=send_sem, recv_sem=root_recv.at[k, s],
            device_id=to(target), device_id_type=MESH)

    def up_copy(k, s):
        return strip_copy(k, s, me + stride, up_send.at[k, s])

    def down_copy(k, s):
        return strip_copy(k, s, me - stride, down_send.at[k, s])

    def along_chain(k):
        return (upper & (k == 0)) | (jnp.logical_not(upper) & (k == total - 1))

    def home_pass(k, s, act):
        @pl.when((k <= home) & (home < total - 1))
        def _():
            act(up_copy(k, s))

        @pl.when((k >= home) & (home > 0))
        def _():
            act(down_copy(k, s))

        for m in range(stride - 1):
            mate = stride * home + lax.rem(lane + 1 + m, stride)
            copy = strip_copy(k, s, mate, mate_send.at[m, k, s])
            if m == 0 and s in DETOUR:
                @pl.when(jnp.logical_not(along_chain(k)))
                def _():
                    act(copy)
            else:
                act(copy)

    def beside_pass(k, s, act):
        if s in DETOUR:
            @pl.when((k == 0) & (home >= total // 2 - 1) & (home < total - 1))
            def _():
                act(up_copy(k, s))

            @pl.when((k == total - 1) & (home <= total // 2) & (home > 0))
            def _():
                act(down_copy(k, s))

    @pl.when(is_home)
    def _():
        def take_rows(part):
            mine_at = pl.ds(pl.multiple_of(me * half, half), half)
            rows[part, mine_at, :] = masked[home, part * half:(part + 1) * half, :]

            @pl.loop(1, n)
            def _(d):
                source = lax.rem(me + d, n)
                row_copy(home, part, source, me).wait_recv()

        def gram_strip(part, at):
            return lax.dot_general(rows[part, :, at], rows[part], (((0,), (0,)), ((), ())),
                                   preferred_element_type=jnp.float32)

        def strips(act, start=0):
            return lax.fori_loop(0, TILES, lambda i, x: act(pl.multiple_of(i * TILE, TILE), x), start)

        def chunks(row0, act, start=0):
            def step(c, x):
                first = pl.multiple_of(c * CHUNK, CHUNK)
                return act(pl.ds(first, CHUNK), pl.ds(pl.multiple_of(row0 + first, CHUNK), CHUNK), x)

            return lax.fori_loop(0, TILE // CHUNK, step, start)

        take_rows(0)

        def first_half(row0, x):
            at = pl.ds(row0, TILE)
            gram[at, :] = gram_strip(0, at)
            return x

        strips(first_half)

        take_rows(1)
        count = count_ref[0]
        for i in range(1, n):
            count = count + count_ref[i]
        inverse = 1.0 / jnp.full((1, 1), count, jnp.int32).astype(jnp.float32)

        def statistic(row0, squares):
            at = pl.ds(row0, TILE)
            product[...] = gram_strip(1, at)

            def step(near, far, squares):
                value = (gram[far, :] + product[near, :]) * inverse
                gram[far, :] = value
                low_a[far, :] = value.astype(jnp.bfloat16)
                value = value * value
                return squares + value[:8] + value[8:]

            squares = chunks(row0, step, squares)
            eye = eye_strip(0, TILE, TILE)
            value = gram[at, at]
            extra = eye * (2.0 * damping * value + damping * damping)
            value = value + damping * eye
            gram[at, at] = value
            low_a[at, at] = value.astype(jnp.bfloat16)
            extra = jnp.sum(extra.reshape(TILE // 8, 8, TILE), axis=0)
            return squares + jnp.concatenate([extra] + [jnp.zeros_like(extra)] * (TILES - 1), axis=1)

        squares = strips(statistic, jnp.zeros((8, BLOCK), jnp.float32))
        squares = jnp.sum(squares, axis=0, keepdims=True)
        scaling = 2.5 / jnp.sqrt(jnp.sum(squares, axis=1, keepdims=True))
        quarter = jnp.sqrt(jnp.sqrt(scaling))

        def second_power(row0, x):
            product[...] = dot(low_a[pl.ds(row0, TILE), :], low_a[...])

            def step(near, far, x):
                second = product[near, :] * (scaling * scaling)
                scaled = gram[far, :] * scaling
                gram[far, :] = scaled
                low_b[far, :] = (0.0625 * second - 0.625 * scaled).astype(jnp.bfloat16)
                value = 1.25 * scaled - 0.25 * second
                wide[far, :] = value
                low_x[far, :] = value.astype(jnp.bfloat16)
                return x

            return chunks(row0, step, x)

        strips(second_power)

        def third_power(row0, x):
            product[...] = dot(low_b[pl.ds(row0, TILE), :], low_x[...])

            def step(near, far, x):
                value = 1.5625 * wide[far, :] + product[near, :]
                wide[far, :] = value
                low_a[far, :] = value.astype(jnp.bfloat16)
                return x

            return chunks(row0, step, x)

        strips(third_power)

        for i in range(TILES):
            at = pl.ds(i * TILE, TILE)
            width = (i + 1) * TILE
            product[:, :width] = dot(low_b[at, :], low_a[:, :width])

            def step(near, far, x, width=width):
                value = 1.5625 * wide[far, :width] + product[near, :width]
                value = quarter * (-0.3125 * gram[far, :width] - 0.25 * value)
                wide[far, :width] = value
                roots[home, far, :width] = value.astype(jnp.bfloat16)
                return x

            chunks(i * TILE, step, 0)
            value = wide[at, at] + quarter * (1.5625 * eye_strip(0, TILE, TILE))
            roots[home, at, at] = value.astype(jnp.bfloat16)
            for s in range(i * TILE // STRIP, (i + 1) * TILE // STRIP):
                home_pass(home, s, lambda copy: copy.start())

    owned_ref[...] = jnp.zeros_like(owned_ref)

    @pl.loop(0, total)
    def _(step):
        k = pick(home * total + step, [p for line in order for p in line])

        @pl.when(jnp.logical_not(is_home & (k == home)))
        def _():
            for s in range(STRIPS):
                strip_copy(k, s, me, up_send.at[k, s]).wait_recv()

                @pl.when(is_home)
                def _():
                    home_pass(k, s, lambda copy: copy.start())

                @pl.when(is_beside)
                def _():
                    beside_pass(k, s, lambda copy: copy.start())

        def mirror(row0, column0, size):
            piece = roots[k, pl.ds(row0, size), pl.ds(column0, size)]
            roots[k, pl.ds(column0, size), pl.ds(row0, size)] = piece.T

        for i in range(TILES):
            mirror(i * TILE + STRIP, i * TILE, STRIP)
            for j in range(i):
                mirror(i * TILE, j * TILE, TILE)
        layer = k // per_device
        column = lax.rem(k, per_device)
        owner = owner_ref[layer, tp * per_device + column]

        @pl.loop(0, TILES)
        def _(i):
            at = pl.ds(pl.multiple_of(i * TILE, TILE), TILE)
            out_at = pl.ds(pl.multiple_of(column * BLOCK + i * TILE, TILE), TILE)
            update_ref[layer, :, out_at] = dot(masked[k], roots[k, :, at]).astype(jnp.bfloat16)
            owned_ref[at, :] = jnp.where(owner == me, roots[k, at, :], owned_ref[at, :])

    each_send(lambda copy: copy.wait_send())

    @pl.loop(0, total)
    def _(k):
        for s in range(STRIPS):
            @pl.when(is_home)
            def _():
                home_pass(k, s, lambda copy: copy.wait_send())

            @pl.when(is_beside)
            def _():
                beside_pass(k, s, lambda copy: copy.wait_send())


def body(n, gradients, row_counts, block_owner):
    layers, row_slots, columns = gradients.shape
    total = layers * (columns // BLOCK)
    stride = n // total
    vmem = pl.BlockSpec(memory_space=pltpu.VMEM)
    smem = pl.BlockSpec(memory_space=pltpu.SMEM)
    square = (BLOCK, BLOCK)
    dma = pltpu.SemaphoreType.DMA
    return pl.pallas_call(
        functools.partial(kernel, n, total),
        out_shape=(
            jax.ShapeDtypeStruct(gradients.shape, jnp.bfloat16),
            jax.ShapeDtypeStruct(square, jnp.bfloat16),
        ),
        in_specs=[smem, smem, vmem],
        out_specs=(vmem, vmem),
        scratch_shapes=[
            pltpu.VMEM((total, row_slots, BLOCK), jnp.bfloat16),
            pltpu.VMEM((2, n * row_slots // 2, BLOCK), jnp.bfloat16),
            pltpu.VMEM(square, jnp.float32),
            pltpu.VMEM(square, jnp.float32),
            pltpu.VMEM((TILE, BLOCK), jnp.float32),
            pltpu.VMEM(square, jnp.bfloat16),
            pltpu.VMEM(square, jnp.bfloat16),
            pltpu.VMEM(square, jnp.bfloat16),
            pltpu.VMEM((total,) + square, jnp.bfloat16),
            dma((total, 2)),
            dma((2, n)),
            dma((total, STRIPS)),
            dma((total, STRIPS)),
            dma((stride - 1, total, STRIPS)),
            dma((total, STRIPS)),
        ],
        compiler_params=pltpu.CompilerParams(
            collective_id=0, has_side_effects=True, vmem_limit_bytes=56 * 2**20
        ),
    )(row_counts, block_owner, gradients)


def solution(mesh):
    placed = (P(None, "fsdp", "tp"), P(), P())
    return jax.shard_map(
        functools.partial(body, mesh.shape["fsdp"]),
        mesh=mesh,
        in_specs=placed,
        out_specs=(P(None, "fsdp", "tp"), P("fsdp", "tp")),
        check_vma=False,
    )
```

```python
import functools

import jax
import jax.numpy as jnp
from jax import lax
from jax.experimental import pallas as pl
from jax.experimental.pallas import tpu as pltpu
from jax.sharding import PartitionSpec as P

BLOCK = 1024
damping = 0.01
TILE = 256
STRIP = 128
STRIPS = BLOCK // STRIP
TILES = BLOCK // TILE
CHUNK = 16
DETOUR = (2, 6, 7)
MESH = pl.DeviceIdType.MESH


def eye_strip(row0, rows, columns):
    row = lax.broadcasted_iota(jnp.int32, (rows, columns), 0) + row0
    column = lax.broadcasted_iota(jnp.int32, (rows, columns), 1)
    return (row == column).astype(jnp.float32)


def dot(a, b):
    return jnp.dot(a, b, preferred_element_type=jnp.float32)


def pick(index, table):
    value = jnp.int32(table[0])
    for i, entry in enumerate(table[1:], 1):
        value = jnp.where(index == i, entry, value)
    return value


def kernel(n, total, count_ref, owner_ref, g_ref, update_ref, owned_ref, masked, rows, gram, wide,
           product, low_a, low_b, low_x, roots, in_send, in_recv, up_send, down_send, mate_send, root_recv):
    me = lax.axis_index("fsdp")
    tp = lax.axis_index("tp")
    layers, row_slots, columns = g_ref.shape
    per_device = columns // BLOCK
    half = row_slots // 2
    stride = n // total
    lane = lax.rem(tp, stride)
    beside = lax.rem(lane + 1, stride)
    home = me // stride
    is_home = lax.rem(me, stride) == lane
    is_beside = lax.rem(me, stride) == beside
    upper = home >= total // 2
    order = [sorted(range(total), key=lambda k: (abs(k - h), k)) for h in range(total)]

    def to(device):
        return {"fsdp": device}

    barrier = pltpu.get_barrier_semaphore()

    @pl.loop(1, n)
    def _(d):
        pl.semaphore_signal(barrier, inc=1, device_id=to(lax.rem(me + d, n)), device_id_type=MESH)

    limit = count_ref[me]

    @pl.loop(0, row_slots // CHUNK)
    def _(c):
        row0 = pl.multiple_of(c * CHUNK, CHUNK)
        at = pl.ds(row0, CHUNK)
        valid = lax.broadcasted_iota(jnp.int32, (CHUNK, BLOCK), 0) + row0 < limit
        valid = jnp.where(valid, 1.0, 0.0).astype(jnp.bfloat16)
        for block in range(total):
            column0 = block % per_device * BLOCK
            masked[block, at, :] = g_ref[block // per_device, at, column0:column0 + BLOCK] * valid

    pl.semaphore_wait(barrier, n - 1)

    def row_copy(block, part, source, target):
        return pltpu.make_async_remote_copy(
            src_ref=masked.at[block, pl.ds(part * half, half)],
            dst_ref=rows.at[part, pl.ds(pl.multiple_of(source * half, half), half)],
            send_sem=in_send.at[block, part],
            recv_sem=in_recv.at[part, source], device_id=to(target), device_id_type=MESH)

    def each_send(act):
        for turn in sorted(range(total), key=lambda d: (min(d, total - d), d)):
            block = lax.rem(home + turn, total)
            target = stride * block + lane

            @pl.when(me != target)
            def _():
                act(block, target)

    def follow(block, target):
        row_copy(block, 0, me, target).wait_send()
        row_copy(block, 1, me, target).start()

    each_send(lambda block, target: row_copy(block, 0, me, target).start())
    each_send(follow)

    def strip_copy(k, s, target, send_sem):
        piece = roots.at[k, pl.ds(s * STRIP, STRIP), pl.ds(0, (s + 1) * STRIP)]
        return pltpu.make_async_remote_copy(
            src_ref=piece, dst_ref=piece, send_sem=send_sem, recv_sem=root_recv.at[k, s],
            device_id=to(target), device_id_type=MESH)

    def up_copy(k, s):
        return strip_copy(k, s, me + stride, up_send.at[k, s])

    def down_copy(k, s):
        return strip_copy(k, s, me - stride, down_send.at[k, s])

    def along_chain(k):
        return (upper & (k == 0)) | (jnp.logical_not(upper) & (k == total - 1))

    def home_pass(k, s, act):
        @pl.when((k <= home) & (home < total - 1))
        def _():
            act(up_copy(k, s))

        @pl.when((k >= home) & (home > 0))
        def _():
            act(down_copy(k, s))

        for m in range(stride - 1):
            mate = stride * home + lax.rem(lane + 1 + m, stride)
            copy = strip_copy(k, s, mate, mate_send.at[m, k, s])
            if m == 0 and s in DETOUR:
                @pl.when(jnp.logical_not(along_chain(k)))
                def _():
                    act(copy)
            else:
                act(copy)

    def beside_pass(k, s, act):
        if s in DETOUR:
            @pl.when((k == 0) & (home >= total // 2 - 1) & (home < total - 1))
            def _():
                act(up_copy(k, s))

            @pl.when((k == total - 1) & (home <= total // 2) & (home > 0))
            def _():
                act(down_copy(k, s))

    @pl.when(is_home)
    def _():
        def take_rows(part):
            mine_at = pl.ds(pl.multiple_of(me * half, half), half)
            rows[part, mine_at, :] = masked[home, part * half:(part + 1) * half, :]

            @pl.loop(1, n)
            def _(d):
                source = lax.rem(me + d, n)
                row_copy(home, part, source, me).wait_recv()

        def gram_strip(part, at):
            return lax.dot_general(rows[part, :, at], rows[part], (((0,), (0,)), ((), ())),
                                   preferred_element_type=jnp.float32)

        def strips(act, start=0):
            return lax.fori_loop(0, TILES, lambda i, x: act(pl.multiple_of(i * TILE, TILE), x), start)

        def chunks(row0, act, start=0):
            def step(c, x):
                first = pl.multiple_of(c * CHUNK, CHUNK)
                return act(pl.ds(first, CHUNK), pl.ds(pl.multiple_of(row0 + first, CHUNK), CHUNK), x)

            return lax.fori_loop(0, TILE // CHUNK, step, start)

        take_rows(0)

        def first_half(row0, x):
            at = pl.ds(row0, TILE)
            gram[at, :] = gram_strip(0, at)
            return x

        strips(first_half)

        take_rows(1)
        count = count_ref[0]
        for i in range(1, n):
            count = count + count_ref[i]
        inverse = 1.0 / jnp.full((1, 1), count, jnp.int32).astype(jnp.float32)

        def statistic(row0, squares):
            at = pl.ds(row0, TILE)
            product[...] = gram_strip(1, at)

            def step(near, far, squares):
                value = (gram[far, :] + product[near, :]) * inverse
                gram[far, :] = value
                low_a[far, :] = value.astype(jnp.bfloat16)
                value = value * value
                return squares + value[:8] + value[8:]

            squares = chunks(row0, step, squares)
            eye = eye_strip(0, TILE, TILE)
            value = gram[at, at]
            extra = eye * (2.0 * damping * value + damping * damping)
            value = value + damping * eye
            gram[at, at] = value
            low_a[at, at] = value.astype(jnp.bfloat16)
            extra = jnp.sum(extra.reshape(TILE // 8, 8, TILE), axis=0)
            return squares + jnp.concatenate([extra] + [jnp.zeros_like(extra)] * (TILES - 1), axis=1)

        squares = strips(statistic, jnp.zeros((8, BLOCK), jnp.float32))
        squares = jnp.sum(squares, axis=0, keepdims=True)
        scaling = 2.5 / jnp.sqrt(jnp.sum(squares, axis=1, keepdims=True))
        quarter = jnp.sqrt(jnp.sqrt(scaling))

        def second_power(row0, x):
            product[...] = dot(low_a[pl.ds(row0, TILE), :], low_a[...])

            def step(near, far, x):
                second = product[near, :] * (scaling * scaling)
                scaled = gram[far, :] * scaling
                gram[far, :] = scaled
                low_b[far, :] = (0.0625 * second - 0.625 * scaled).astype(jnp.bfloat16)
                value = 1.25 * scaled - 0.25 * second
                wide[far, :] = value
                low_x[far, :] = value.astype(jnp.bfloat16)
                return x

            return chunks(row0, step, x)

        strips(second_power)

        def third_power(row0, x):
            product[...] = dot(low_b[pl.ds(row0, TILE), :], low_x[...])

            def step(near, far, x):
                value = 1.5625 * wide[far, :] + product[near, :]
                wide[far, :] = value
                low_a[far, :] = value.astype(jnp.bfloat16)
                return x

            return chunks(row0, step, x)

        strips(third_power)

        for i in range(TILES):
            at = pl.ds(i * TILE, TILE)
            width = (i + 1) * TILE
            product[:, :width] = dot(low_b[at, :], low_a[:, :width])

            def step(near, far, x, width=width):
                value = 1.5625 * wide[far, :width] + product[near, :width]
                value = quarter * (-0.3125 * gram[far, :width] - 0.25 * value)
                wide[far, :width] = value
                roots[home, far, :width] = value.astype(jnp.bfloat16)
                return x

            chunks(i * TILE, step, 0)
            value = wide[at, at] + quarter * (1.5625 * eye_strip(0, TILE, TILE))
            roots[home, at, at] = value.astype(jnp.bfloat16)
            for s in range(i * TILE // STRIP, (i + 1) * TILE // STRIP):
                home_pass(home, s, lambda copy: copy.start())

    owned_ref[...] = jnp.zeros_like(owned_ref)

    @pl.loop(0, total)
    def _(step):
        k = pick(home * total + step, [p for line in order for p in line])

        for s in range(STRIPS):
            @pl.when(jnp.logical_not(is_home & (k == home)))
            def _():
                strip_copy(k, s, me, up_send.at[k, s]).wait_recv()

                @pl.when(is_home)
                def _():
                    home_pass(k, s, lambda copy: copy.start())

                @pl.when(is_beside)
                def _():
                    beside_pass(k, s, lambda copy: copy.start())

            row0 = s * STRIP
            if s > 0:
                roots[k, :row0, row0:row0 + STRIP] = roots[k, row0:row0 + STRIP, :row0].T

        layer = k // per_device
        column = lax.rem(k, per_device)
        owner = owner_ref[layer, tp * per_device + column]

        @pl.loop(0, TILES)
        def _(i):
            at = pl.ds(pl.multiple_of(i * TILE, TILE), TILE)
            out_at = pl.ds(pl.multiple_of(column * BLOCK + i * TILE, TILE), TILE)
            update_ref[layer, :, out_at] = dot(masked[k], roots[k, :, at]).astype(jnp.bfloat16)
            owned_ref[at, :] = jnp.where(owner == me, roots[k, at, :], owned_ref[at, :])

    each_send(lambda block, target: row_copy(block, 1, me, target).wait_send())

    @pl.loop(0, total)
    def _(k):
        for s in range(STRIPS):
            @pl.when(is_home)
            def _():
                home_pass(k, s, lambda copy: copy.wait_send())

            @pl.when(is_beside)
            def _():
                beside_pass(k, s, lambda copy: copy.wait_send())


def body(n, gradients, row_counts, block_owner):
    layers, row_slots, columns = gradients.shape
    total = layers * (columns // BLOCK)
    stride = n // total
    vmem = pl.BlockSpec(memory_space=pltpu.VMEM)
    smem = pl.BlockSpec(memory_space=pltpu.SMEM)
    square = (BLOCK, BLOCK)
    dma = pltpu.SemaphoreType.DMA
    row_bytes = 2 * row_slots * BLOCK
    square_bytes = 2 * BLOCK * BLOCK
    held = (n + 3 * total) * row_bytes + (total + 8) * square_bytes + TILE * BLOCK * 4
    return pl.pallas_call(
        functools.partial(kernel, n, total),
        out_shape=(
            jax.ShapeDtypeStruct(gradients.shape, jnp.bfloat16),
            jax.ShapeDtypeStruct(square, jnp.bfloat16),
        ),
        in_specs=[smem, smem, vmem],
        out_specs=(vmem, vmem),
        scratch_shapes=[
            pltpu.VMEM((total, row_slots, BLOCK), jnp.bfloat16),
            pltpu.VMEM((2, n * row_slots // 2, BLOCK), jnp.bfloat16),
            pltpu.VMEM(square, jnp.float32),
            pltpu.VMEM(square, jnp.float32),
            pltpu.VMEM((TILE, BLOCK), jnp.float32),
            pltpu.VMEM(square, jnp.bfloat16),
            pltpu.VMEM(square, jnp.bfloat16),
            pltpu.VMEM(square, jnp.bfloat16),
            pltpu.VMEM((total,) + square, jnp.bfloat16),
            dma((total, 2)),
            dma((2, n)),
            dma((total, STRIPS)),
            dma((total, STRIPS)),
            dma((stride - 1, total, STRIPS)),
            dma((total, STRIPS)),
        ],
        compiler_params=pltpu.CompilerParams(
            collective_id=0, has_side_effects=True, vmem_limit_bytes=held + 6 * 2**20
        ),
    )(row_counts, block_owner, gradients)


def solution(mesh):
    placed = (P(None, "fsdp", "tp"), P(), P())
    return jax.shard_map(
        functools.partial(body, mesh.shape["fsdp"]),
        mesh=mesh,
        in_specs=placed,
        out_specs=(P(None, "fsdp", "tp"), P("fsdp", "tp")),
        check_vma=False,
    )
```

```python
import functools

import jax
import jax.numpy as jnp
from jax import lax
from jax.experimental import pallas as pl
from jax.experimental.pallas import tpu as pltpu
from jax.sharding import PartitionSpec as P

BLOCK = 1024
damping = 0.01
TILE = 256
STRIP = 64
STRIPS = BLOCK // STRIP
TILES = BLOCK // TILE
LANES = 128
CHUNK = 16
DETOUR = (4, 5, 12, 13, 14, 15)
MESH = pl.DeviceIdType.MESH


def eye_strip(row0, rows, columns):
    row = lax.broadcasted_iota(jnp.int32, (rows, columns), 0) + row0
    column = lax.broadcasted_iota(jnp.int32, (rows, columns), 1)
    return (row == column).astype(jnp.float32)


def dot(a, b):
    return jnp.dot(a, b, preferred_element_type=jnp.float32)


def pick(index, table):
    value = jnp.int32(table[0])
    for i, entry in enumerate(table[1:], 1):
        value = jnp.where(index == i, entry, value)
    return value


def kernel(n, total, count_ref, owner_ref, g_ref, update_ref, owned_ref, masked, rows, gram, wide,
           product, low_a, low_b, low_x, roots, in_send, in_recv, up_send, down_send, mate_send, root_recv):
    me = lax.axis_index("fsdp")
    tp = lax.axis_index("tp")
    layers, row_slots, columns = g_ref.shape
    per_device = columns // BLOCK
    half = row_slots // 2
    stride = n // total
    lane = lax.rem(tp, stride)
    beside = lax.rem(lane + 1, stride)
    home = me // stride
    is_home = lax.rem(me, stride) == lane
    is_beside = lax.rem(me, stride) == beside
    upper = home >= total // 2
    order = [sorted(range(total), key=lambda k: (abs(k - h), k)) for h in range(total)]

    def to(device):
        return {"fsdp": device}

    barrier = pltpu.get_barrier_semaphore()

    @pl.loop(1, n)
    def _(d):
        pl.semaphore_signal(barrier, inc=1, device_id=to(lax.rem(me + d, n)), device_id_type=MESH)

    limit = count_ref[me]

    @pl.loop(0, row_slots // CHUNK)
    def _(c):
        row0 = pl.multiple_of(c * CHUNK, CHUNK)
        at = pl.ds(row0, CHUNK)
        valid = lax.broadcasted_iota(jnp.int32, (CHUNK, BLOCK), 0) + row0 < limit
        valid = jnp.where(valid, 1.0, 0.0).astype(jnp.bfloat16)
        for block in range(total):
            column0 = block % per_device * BLOCK
            masked[block, at, :] = g_ref[block // per_device, at, column0:column0 + BLOCK] * valid

    pl.semaphore_wait(barrier, n - 1)

    def row_copy(block, part, source, target):
        return pltpu.make_async_remote_copy(
            src_ref=masked.at[block, pl.ds(part * half, half)],
            dst_ref=rows.at[part, pl.ds(pl.multiple_of(source * half, half), half)],
            send_sem=in_send.at[block, part],
            recv_sem=in_recv.at[part, source], device_id=to(target), device_id_type=MESH)

    def each_send(act):
        for turn in sorted(range(total), key=lambda d: (min(d, total - d), d)):
            block = lax.rem(home + turn, total)
            target = stride * block + lane

            @pl.when(me != target)
            def _():
                act(block, target)

    def follow(block, target):
        row_copy(block, 0, me, target).wait_send()
        row_copy(block, 1, me, target).start()

    each_send(lambda block, target: row_copy(block, 0, me, target).start())
    each_send(follow)

    def strip_copy(k, s, target, send_sem):
        piece = roots.at[k, pl.ds(s * STRIP, STRIP), pl.ds(0, ((s + 1) * STRIP + LANES - 1) // LANES * LANES)]
        return pltpu.make_async_remote_copy(
            src_ref=piece, dst_ref=piece, send_sem=send_sem, recv_sem=root_recv.at[k, s],
            device_id=to(target), device_id_type=MESH)

    def up_copy(k, s):
        return strip_copy(k, s, me + stride, up_send.at[k, s])

    def down_copy(k, s):
        return strip_copy(k, s, me - stride, down_send.at[k, s])

    def along_chain(k):
        return (upper & (k == 0)) | (jnp.logical_not(upper) & (k == total - 1))

    def home_pass(k, s, act):
        @pl.when((k <= home) & (home < total - 1))
        def _():
            act(up_copy(k, s))

        @pl.when((k >= home) & (home > 0))
        def _():
            act(down_copy(k, s))

        for m in range(stride - 1):
            mate = stride * home + lax.rem(lane + 1 + m, stride)
            copy = strip_copy(k, s, mate, mate_send.at[m, k, s])
            if m == 0 and s in DETOUR:
                @pl.when(jnp.logical_not(along_chain(k)))
                def _():
                    act(copy)
            else:
                act(copy)

    def beside_pass(k, s, act):
        if s in DETOUR:
            @pl.when((k == 0) & (home >= total // 2 - 1) & (home < total - 1))
            def _():
                act(up_copy(k, s))

            @pl.when((k == total - 1) & (home <= total // 2) & (home > 0))
            def _():
                act(down_copy(k, s))

    @pl.when(is_home)
    def _():
        def take_rows(part):
            mine_at = pl.ds(pl.multiple_of(me * half, half), half)
            rows[part, mine_at, :] = masked[home, part * half:(part + 1) * half, :]

            @pl.loop(1, n)
            def _(d):
                source = lax.rem(me + d, n)
                row_copy(home, part, source, me).wait_recv()

        def gram_strip(part, at):
            return lax.dot_general(rows[part, :, at], rows[part], (((0,), (0,)), ((), ())),
                                   preferred_element_type=jnp.float32)

        def strips(act, start=0):
            return lax.fori_loop(0, TILES, lambda i, x: act(pl.multiple_of(i * TILE, TILE), x), start)

        def chunks(row0, act, start=0):
            def step(c, x):
                first = pl.multiple_of(c * CHUNK, CHUNK)
                return act(pl.ds(first, CHUNK), pl.ds(pl.multiple_of(row0 + first, CHUNK), CHUNK), x)

            return lax.fori_loop(0, TILE // CHUNK, step, start)

        take_rows(0)

        def first_half(row0, x):
            at = pl.ds(row0, TILE)
            gram[at, :] = gram_strip(0, at)
            return x

        strips(first_half)

        take_rows(1)
        count = count_ref[0]
        for i in range(1, n):
            count = count + count_ref[i]
        inverse = 1.0 / jnp.full((1, 1), count, jnp.int32).astype(jnp.float32)

        def statistic(row0, squares):
            at = pl.ds(row0, TILE)
            product[...] = gram_strip(1, at)

            def step(near, far, squares):
                value = (gram[far, :] + product[near, :]) * inverse
                gram[far, :] = value
                low_a[far, :] = value.astype(jnp.bfloat16)
                value = value * value
                return squares + value[:8] + value[8:]

            squares = chunks(row0, step, squares)
            eye = eye_strip(0, TILE, TILE)
            value = gram[at, at]
            extra = eye * (2.0 * damping * value + damping * damping)
            value = value + damping * eye
            gram[at, at] = value
            low_a[at, at] = value.astype(jnp.bfloat16)
            extra = jnp.sum(extra.reshape(TILE // 8, 8, TILE), axis=0)
            return squares + jnp.concatenate([extra] + [jnp.zeros_like(extra)] * (TILES - 1), axis=1)

        squares = strips(statistic, jnp.zeros((8, BLOCK), jnp.float32))
        squares = jnp.sum(squares, axis=0, keepdims=True)
        scaling = 2.5 / jnp.sqrt(jnp.sum(squares, axis=1, keepdims=True))
        quarter = jnp.sqrt(jnp.sqrt(scaling))

        def second_power(row0, x):
            product[...] = dot(low_a[pl.ds(row0, TILE), :], low_a[...])

            def step(near, far, x):
                second = product[near, :] * (scaling * scaling)
                scaled = gram[far, :] * scaling
                gram[far, :] = scaled
                low_b[far, :] = (0.0625 * second - 0.625 * scaled).astype(jnp.bfloat16)
                value = 1.25 * scaled - 0.25 * second
                wide[far, :] = value
                low_x[far, :] = value.astype(jnp.bfloat16)
                return x

            return chunks(row0, step, x)

        strips(second_power)

        def third_power(row0, x):
            product[...] = dot(low_b[pl.ds(row0, TILE), :], low_x[...])

            def step(near, far, x):
                value = 1.5625 * wide[far, :] + product[near, :]
                wide[far, :] = value
                low_a[far, :] = value.astype(jnp.bfloat16)
                return x

            return chunks(row0, step, x)

        strips(third_power)

        for i in range(TILES):
            at = pl.ds(i * TILE, TILE)
            width = (i + 1) * TILE
            product[:, :width] = dot(low_b[at, :], low_a[:, :width])

            def step(near, far, x, width=width):
                value = 1.5625 * wide[far, :width] + product[near, :width]
                value = quarter * (-0.3125 * gram[far, :width] - 0.25 * value)
                wide[far, :width] = value
                roots[home, far, :width] = value.astype(jnp.bfloat16)
                return x

            chunks(i * TILE, step, 0)
            value = wide[at, at] + quarter * (1.5625 * eye_strip(0, TILE, TILE))
            roots[home, at, at] = value.astype(jnp.bfloat16)
            for s in range(i * TILE // STRIP, (i + 1) * TILE // STRIP):
                home_pass(home, s, lambda copy: copy.start())

    owned_ref[...] = jnp.zeros_like(owned_ref)

    @pl.loop(0, total)
    def _(step):
        k = pick(home * total + step, [p for line in order for p in line])

        for s in range(STRIPS):
            @pl.when(jnp.logical_not(is_home & (k == home)))
            def _():
                strip_copy(k, s, me, up_send.at[k, s]).wait_recv()

                @pl.when(is_home)
                def _():
                    home_pass(k, s, lambda copy: copy.start())

                @pl.when(is_beside)
                def _():
                    beside_pass(k, s, lambda copy: copy.start())

            row0 = (s + 1) * STRIP - LANES
            if row0 > 0 and row0 % LANES == 0:
                roots[k, :row0, row0:row0 + LANES] = roots[k, row0:row0 + LANES, :row0].T

        layer = k // per_device
        column = lax.rem(k, per_device)
        owner = owner_ref[layer, tp * per_device + column]

        @pl.loop(0, TILES)
        def _(i):
            at = pl.ds(pl.multiple_of(i * TILE, TILE), TILE)
            out_at = pl.ds(pl.multiple_of(column * BLOCK + i * TILE, TILE), TILE)
            update_ref[layer, :, out_at] = dot(masked[k], roots[k, :, at]).astype(jnp.bfloat16)
            owned_ref[at, :] = jnp.where(owner == me, roots[k, at, :], owned_ref[at, :])

    each_send(lambda block, target: row_copy(block, 1, me, target).wait_send())

    @pl.loop(0, total)
    def _(k):
        for s in range(STRIPS):
            @pl.when(is_home)
            def _():
                home_pass(k, s, lambda copy: copy.wait_send())

            @pl.when(is_beside)
            def _():
                beside_pass(k, s, lambda copy: copy.wait_send())


def body(n, gradients, row_counts, block_owner):
    layers, row_slots, columns = gradients.shape
    total = layers * (columns // BLOCK)
    stride = n // total
    vmem = pl.BlockSpec(memory_space=pltpu.VMEM)
    smem = pl.BlockSpec(memory_space=pltpu.SMEM)
    square = (BLOCK, BLOCK)
    dma = pltpu.SemaphoreType.DMA
    row_bytes = 2 * row_slots * BLOCK
    square_bytes = 2 * BLOCK * BLOCK
    held = (n + 3 * total) * row_bytes + (total + 8) * square_bytes + TILE * BLOCK * 4
    return pl.pallas_call(
        functools.partial(kernel, n, total),
        out_shape=(
            jax.ShapeDtypeStruct(gradients.shape, jnp.bfloat16),
            jax.ShapeDtypeStruct(square, jnp.bfloat16),
        ),
        in_specs=[smem, smem, vmem],
        out_specs=(vmem, vmem),
        scratch_shapes=[
            pltpu.VMEM((total, row_slots, BLOCK), jnp.bfloat16),
            pltpu.VMEM((2, n * row_slots // 2, BLOCK), jnp.bfloat16),
            pltpu.VMEM(square, jnp.float32),
            pltpu.VMEM(square, jnp.float32),
            pltpu.VMEM((TILE, BLOCK), jnp.float32),
            pltpu.VMEM(square, jnp.bfloat16),
            pltpu.VMEM(square, jnp.bfloat16),
            pltpu.VMEM(square, jnp.bfloat16),
            pltpu.VMEM((total,) + square, jnp.bfloat16),
            dma((total, 2)),
            dma((2, n)),
            dma((total, STRIPS)),
            dma((total, STRIPS)),
            dma((stride - 1, total, STRIPS)),
            dma((total, STRIPS)),
        ],
        compiler_params=pltpu.CompilerParams(
            collective_id=0, has_side_effects=True, vmem_limit_bytes=held + 6 * 2**20
        ),
    )(row_counts, block_owner, gradients)


def solution(mesh):
    placed = (P(None, "fsdp", "tp"), P(), P())
    return jax.shard_map(
        functools.partial(body, mesh.shape["fsdp"]),
        mesh=mesh,
        in_specs=placed,
        out_specs=(P(None, "fsdp", "tp"), P("fsdp", "tp")),
        check_vma=False,
    )
```

```python
import functools

import jax
import jax.numpy as jnp
from jax import lax
from jax.experimental import pallas as pl
from jax.experimental.pallas import tpu as pltpu
from jax.sharding import PartitionSpec as P

BLOCK = 1024
damping = 0.01
TILE = 256
STRIP = 128
STRIPS = BLOCK // STRIP
TILES = BLOCK // TILE
CHUNK = 16
DETOUR = (2, 6, 7)
MESH = pl.DeviceIdType.MESH


def eye_strip(row0, rows, columns):
    row = lax.broadcasted_iota(jnp.int32, (rows, columns), 0) + row0
    column = lax.broadcasted_iota(jnp.int32, (rows, columns), 1)
    return (row == column).astype(jnp.float32)


def dot(a, b):
    return jnp.dot(a, b, preferred_element_type=jnp.float32)


def pick(index, table):
    value = jnp.int32(table[0])
    for i, entry in enumerate(table[1:], 1):
        value = jnp.where(index == i, entry, value)
    return value


def kernel(n, total, count_ref, owner_ref, g_ref, update_ref, owned_ref, masked, rows, gram, wide,
           product, low_a, low_b, low_x, roots, in_send, in_recv, up_send, down_send, mate_send, root_recv):
    me = lax.axis_index("fsdp")
    tp = lax.axis_index("tp")
    layers, row_slots, columns = g_ref.shape
    per_device = columns // BLOCK
    half = row_slots // 2
    stride = n // total
    lane = lax.rem(tp, stride)
    beside = lax.rem(lane + 1, stride)
    home = me // stride
    is_home = lax.rem(me, stride) == lane
    is_beside = lax.rem(me, stride) == beside
    upper = home >= total // 2
    order = [sorted(range(total), key=lambda k: (abs(k - h), k)) for h in range(total)]

    def to(device):
        return {"fsdp": device}

    barrier = pltpu.get_barrier_semaphore()

    @pl.loop(1, n)
    def _(d):
        pl.semaphore_signal(barrier, inc=1, device_id=to(lax.rem(me + d, n)), device_id_type=MESH)

    limit = count_ref[me]

    @pl.loop(0, row_slots // CHUNK)
    def _(c):
        row0 = pl.multiple_of(c * CHUNK, CHUNK)
        at = pl.ds(row0, CHUNK)
        valid = lax.broadcasted_iota(jnp.int32, (CHUNK, BLOCK), 0) + row0 < limit
        valid = jnp.where(valid, 1.0, 0.0).astype(jnp.bfloat16)
        for block in range(total):
            column0 = block % per_device * BLOCK
            masked[block, at, :] = g_ref[block // per_device, at, column0:column0 + BLOCK] * valid

    pl.semaphore_wait(barrier, n - 1)

    def row_copy(block, part, source, target):
        return pltpu.make_async_remote_copy(
            src_ref=masked.at[block, pl.ds(part * half, half)],
            dst_ref=rows.at[part, pl.ds(pl.multiple_of(source * half, half), half)],
            send_sem=in_send.at[block, part],
            recv_sem=in_recv.at[part, source], device_id=to(target), device_id_type=MESH)

    def each_send(act):
        for turn in sorted(range(total), key=lambda d: (min(d, total - d), d)):
            block = lax.rem(home + turn, total)
            target = stride * block + lane

            @pl.when(me != target)
            def _():
                act(block, target)

    def follow(block, target):
        row_copy(block, 0, me, target).wait_send()
        row_copy(block, 1, me, target).start()

    each_send(lambda block, target: row_copy(block, 0, me, target).start())
    each_send(follow)

    def strip_copy(k, s, target, send_sem):
        piece = roots.at[k, pl.ds(s * STRIP, STRIP), pl.ds(0, (s + 1) * STRIP)]
        return pltpu.make_async_remote_copy(
            src_ref=piece, dst_ref=piece, send_sem=send_sem, recv_sem=root_recv.at[k, s],
            device_id=to(target), device_id_type=MESH)

    def up_copy(k, s):
        return strip_copy(k, s, me + stride, up_send.at[k, s])

    def down_copy(k, s):
        return strip_copy(k, s, me - stride, down_send.at[k, s])

    def along_chain(k):
        return (upper & (k == 0)) | (jnp.logical_not(upper) & (k == total - 1))

    def home_pass(k, s, act):
        @pl.when((k <= home) & (home < total - 1))
        def _():
            act(up_copy(k, s))

        @pl.when((k >= home) & (home > 0))
        def _():
            act(down_copy(k, s))

        for m in range(stride - 1):
            mate = stride * home + lax.rem(lane + 1 + m, stride)
            copy = strip_copy(k, s, mate, mate_send.at[m, k, s])
            if m == 0 and s in DETOUR:
                @pl.when(jnp.logical_not(along_chain(k)))
                def _():
                    act(copy)
            else:
                act(copy)

    def beside_pass(k, s, act):
        if s in DETOUR:
            @pl.when((k == 0) & (home >= total // 2 - 1) & (home < total - 1))
            def _():
                act(up_copy(k, s))

            @pl.when((k == total - 1) & (home <= total // 2) & (home > 0))
            def _():
                act(down_copy(k, s))

    @pl.when(is_home)
    def _():
        def take_rows(part):
            mine_at = pl.ds(pl.multiple_of(me * half, half), half)
            rows[part, mine_at, :] = masked[home, part * half:(part + 1) * half, :]

            @pl.loop(1, n)
            def _(d):
                source = lax.rem(me + d, n)
                row_copy(home, part, source, me).wait_recv()

        def gram_strip(part, at):
            return lax.dot_general(rows[part, :, at], rows[part], (((0,), (0,)), ((), ())),
                                   preferred_element_type=jnp.float32)

        def strips(act, start=0):
            return lax.fori_loop(0, TILES, lambda i, x: act(pl.multiple_of(i * TILE, TILE), x), start)

        def chunks(row0, act, start=0):
            def step(c, x):
                first = pl.multiple_of(c * CHUNK, CHUNK)
                return act(pl.ds(first, CHUNK), pl.ds(pl.multiple_of(row0 + first, CHUNK), CHUNK), x)

            return lax.fori_loop(0, TILE // CHUNK, step, start)

        take_rows(0)

        def first_half(row0, x):
            at = pl.ds(row0, TILE)
            gram[at, :] = gram_strip(0, at)
            return x

        strips(first_half)

        take_rows(1)
        count = count_ref[0]
        for i in range(1, n):
            count = count + count_ref[i]
        inverse = 1.0 / jnp.full((1, 1), count, jnp.int32).astype(jnp.float32)

        def statistic(row0, squares):
            at = pl.ds(row0, TILE)
            product[...] = gram_strip(1, at)

            def step(near, far, squares):
                value = (gram[far, :] + product[near, :]) * inverse
                gram[far, :] = value
                low_a[far, :] = value.astype(jnp.bfloat16)
                value = value * value
                return squares + value[:8] + value[8:]

            squares = chunks(row0, step, squares)
            eye = eye_strip(0, TILE, TILE)
            value = gram[at, at]
            extra = eye * (2.0 * damping * value + damping * damping)
            value = value + damping * eye
            gram[at, at] = value
            low_a[at, at] = value.astype(jnp.bfloat16)
            extra = jnp.sum(extra.reshape(TILE // 8, 8, TILE), axis=0)
            return squares + jnp.concatenate([extra] + [jnp.zeros_like(extra)] * (TILES - 1), axis=1)

        squares = strips(statistic, jnp.zeros((8, BLOCK), jnp.float32))
        squares = jnp.sum(squares, axis=0, keepdims=True)
        scaling = 2.5 / jnp.sqrt(jnp.sum(squares, axis=1, keepdims=True))
        quarter = jnp.sqrt(jnp.sqrt(scaling))

        def second_power(row0, x):
            product[...] = dot(low_a[pl.ds(row0, TILE), :], low_a[...])

            def step(near, far, x):
                second = product[near, :] * (scaling * scaling)
                scaled = gram[far, :] * scaling
                gram[far, :] = scaled
                low_b[far, :] = (0.0625 * second - 0.625 * scaled).astype(jnp.bfloat16)
                value = 1.25 * scaled - 0.25 * second
                wide[far, :] = value
                low_x[far, :] = value.astype(jnp.bfloat16)
                return x

            return chunks(row0, step, x)

        strips(second_power)

        def third_power(row0, x):
            product[...] = dot(low_b[pl.ds(row0, TILE), :], low_x[...])

            def step(near, far, x):
                value = 1.5625 * wide[far, :] + product[near, :]
                wide[far, :] = value
                low_a[far, :] = value.astype(jnp.bfloat16)
                return x

            return chunks(row0, step, x)

        strips(third_power)

        for i in range(TILES):
            at = pl.ds(i * TILE, TILE)
            width = (i + 1) * TILE
            product[:, :width] = dot(low_b[at, :], low_a[:, :width])

            def step(near, far, x, width=width):
                value = 1.5625 * wide[far, :width] + product[near, :width]
                value = quarter * (-0.3125 * gram[far, :width] - 0.25 * value)
                wide[far, :width] = value
                roots[home, far, :width] = value.astype(jnp.bfloat16)
                return x

            chunks(i * TILE, step, 0)
            value = wide[at, at] + quarter * (1.5625 * eye_strip(0, TILE, TILE))
            roots[home, at, at] = value.astype(jnp.bfloat16)
            for s in range(i * TILE // STRIP, (i + 1) * TILE // STRIP):
                home_pass(home, s, lambda copy: copy.start())

    owned_ref[...] = jnp.zeros_like(owned_ref)

    def kth(step):
        return pick(home * total + step, [p for line in order for p in line])

    @pl.loop(0, total)
    def _(step):
        k = kth(step)

        for s in range(STRIPS):
            @pl.when(jnp.logical_not(is_home & (k == home)))
            def _():
                strip_copy(k, s, me, up_send.at[k, s]).wait_recv()

                @pl.when(is_home)
                def _():
                    home_pass(k, s, lambda copy: copy.start())

                @pl.when(is_beside)
                def _():
                    beside_pass(k, s, lambda copy: copy.start())

            row0 = s * STRIP
            if s > 0:
                roots[k, :row0, row0:row0 + STRIP] = roots[k, row0:row0 + STRIP, :row0].T

        @pl.loop(jnp.where(step == 1, 0, step), jnp.where(step == 0, 0, step + 1))
        def _(done):
            k = kth(done)
            layer = k // per_device
            column = lax.rem(k, per_device)
            owner = owner_ref[layer, tp * per_device + column]

            @pl.loop(0, TILES)
            def _(i):
                at = pl.ds(pl.multiple_of(i * TILE, TILE), TILE)
                out_at = pl.ds(pl.multiple_of(column * BLOCK + i * TILE, TILE), TILE)
                update_ref[layer, :, out_at] = dot(masked[k], roots[k, :, at]).astype(jnp.bfloat16)
                owned_ref[at, :] = jnp.where(owner == me, roots[k, at, :], owned_ref[at, :])

    each_send(lambda block, target: row_copy(block, 1, me, target).wait_send())

    @pl.loop(0, total)
    def _(k):
        for s in range(STRIPS):
            @pl.when(is_home)
            def _():
                home_pass(k, s, lambda copy: copy.wait_send())

            @pl.when(is_beside)
            def _():
                beside_pass(k, s, lambda copy: copy.wait_send())


def body(n, gradients, row_counts, block_owner):
    layers, row_slots, columns = gradients.shape
    total = layers * (columns // BLOCK)
    stride = n // total
    vmem = pl.BlockSpec(memory_space=pltpu.VMEM)
    smem = pl.BlockSpec(memory_space=pltpu.SMEM)
    square = (BLOCK, BLOCK)
    dma = pltpu.SemaphoreType.DMA
    row_bytes = 2 * row_slots * BLOCK
    square_bytes = 2 * BLOCK * BLOCK
    held = (n + 3 * total) * row_bytes + (total + 8) * square_bytes + TILE * BLOCK * 4
    return pl.pallas_call(
        functools.partial(kernel, n, total),
        out_shape=(
            jax.ShapeDtypeStruct(gradients.shape, jnp.bfloat16),
            jax.ShapeDtypeStruct(square, jnp.bfloat16),
        ),
        in_specs=[smem, smem, vmem],
        out_specs=(vmem, vmem),
        scratch_shapes=[
            pltpu.VMEM((total, row_slots, BLOCK), jnp.bfloat16),
            pltpu.VMEM((2, n * row_slots // 2, BLOCK), jnp.bfloat16),
            pltpu.VMEM(square, jnp.float32),
            pltpu.VMEM(square, jnp.float32),
            pltpu.VMEM((TILE, BLOCK), jnp.float32),
            pltpu.VMEM(square, jnp.bfloat16),
            pltpu.VMEM(square, jnp.bfloat16),
            pltpu.VMEM(square, jnp.bfloat16),
            pltpu.VMEM((total,) + square, jnp.bfloat16),
            dma((total, 2)),
            dma((2, n)),
            dma((total, STRIPS)),
            dma((total, STRIPS)),
            dma((stride - 1, total, STRIPS)),
            dma((total, STRIPS)),
        ],
        compiler_params=pltpu.CompilerParams(
            collective_id=0, has_side_effects=True, vmem_limit_bytes=held + 6 * 2**20
        ),
    )(row_counts, block_owner, gradients)


def solution(mesh):
    placed = (P(None, "fsdp", "tp"), P(), P())
    return jax.shard_map(
        functools.partial(body, mesh.shape["fsdp"]),
        mesh=mesh,
        in_specs=placed,
        out_specs=(P(None, "fsdp", "tp"), P("fsdp", "tp")),
        check_vma=False,
    )
```
